512 devices in a mesh: dp: 8 (over y_hi, core), width: 8 (over z), hidden: 8 (over y_lo, x).
Axes of the slice: x: 4, y: 8 (y_hi: 4, y_lo: 2; y = y_hi * 2 + y_lo), z: 8, core: 2. Of those that a mesh axis runs over, the one named last changes fastest.
Arguments:
- tokens: bfloat16 [1024, 4096], P('dp', 'width'), may hold values from -6 to 6
- token_job_index: int32 [1024], P('dp'), may hold values from 0 to 15, as said below
- gate_up_matrix: bfloat16 [2, 4096, 14336], P(None, 'width', ('dp', 'hidden')), may hold values from -0.09375 to 0.09375
- down_matrix: bfloat16 [14336, 4096], P(('dp', 'hidden'), 'width'), may hold values from -0.125 to 0.125
- adapter_input_maps: bfloat16 [2, 4096, 256], P(None, 'width'), may hold values from -0.09375 to 0.09375
- adapter_output_maps: bfloat16 [2, 256, 14336], P(None, None, ('dp', 'hidden')), may hold values from -1.5 to 1.5
- cotangent: bfloat16 [1024, 4096], P('dp', ('width', 'hidden')), may hold values from -6 to 6
Outputs:
- mixed: bfloat16 [1024, 4096], P('dp', ('width', 'hidden'))
- input_gradient: bfloat16 [1024, 4096], P('dp', ('width', 'hidden'))
- adapter_input_gradient: float32 [2, 4096, 256], P(None, 'width')
- adapter_output_gradient: float32 [2, 256, 14336], P(None, None, ('dp', 'hidden'))
The draws below stay inside these ranges and needn't reach their ends.
Inputs may be any that keep to these rules, and one draw needn't show every extreme that they name: `token_job_index`: constant on aligned blocks of 128 tokens; 0 and 15 occur in every draw.
All inputs are finite; a program needn't handle non-finite values.
Results may differ from the reference program's by a relative error of at most 0.014.
Values may be sent and summed in bfloat16 or wider, within the bound.
A program may use at most 64 MiB of HBM per device.

```python
import jax
import jax.numpy as jnp
from jax import lax

MODEL_FEATURES = 4096
HIDDEN_UNITS = 14336
JOB_COUNT = 16
ADAPTER_RANK = 16
JOB_ROWS = 128
TOKENS = 1024


def draw_token_job_index(key, part):
    key = jax.random.fold_in(key, 11)
    block_count = TOKENS // JOB_ROWS
    first_key = jax.random.fold_in(key, 1)
    second_key = jax.random.fold_in(key, 2)
    third_key = jax.random.fold_in(key, 3)
    block_jobs = jax.random.randint(first_key, (block_count,), 0, JOB_COUNT)
    low_place = jax.random.randint(second_key, (), 0, block_count)
    high_place = (low_place + 1 + jax.random.randint(third_key, (), 0, block_count - 1)) % block_count
    block_jobs = block_jobs.at[low_place].set(0)
    block_jobs = block_jobs.at[high_place].set(JOB_COUNT - 1)
    return jnp.repeat(block_jobs, JOB_ROWS, total_repeat_length=TOKENS).astype(jnp.int32)


def strengthened(result, stream_key, source, target, shards_of, factor):
    owner, partner = [(jnp.arange(result.shape[axis_at]) // (result.shape[axis_at] // shards_of)).reshape([-1 if axis == axis_at else 1 for axis in range(result.ndim)]) for axis_at in (source, target)]
    chosen = jax.random.permutation(stream_key, shards_of)[partner]
    strong = (owner == chosen) | (owner == (partner + shards_of // 2) % shards_of)
    return jnp.where(strong, factor * result, result)


def levels(stream_key, extent, split, least, largest):
    gain, own = 1.0, jax.random.fold_in(stream_key, 6)
    for dim, blocks in split:
        draws = jnp.exp(jax.random.uniform(jax.random.fold_in(own, dim), (blocks,), jnp.float32, least / len(split), largest / len(split)))
        gain = gain * jnp.repeat(draws, extent[dim] // blocks).reshape([-1 if axis == dim else 1 for axis in range(len(extent))])
    return gain


def normal_values(key, extent, deviation, most, split=(), kind=jnp.bfloat16):
    drawn = deviation * jax.random.normal(key, extent, jnp.float32)
    if split:
        drawn = drawn * levels(key, extent, split, -0.22, 0.18)
    return jnp.clip(drawn, -most, most).astype(kind)


def heavy_noise(key, shape, deviation, most, shards, heavy, kind=jnp.bfloat16):
    result = deviation * jax.random.normal(key, shape, jnp.float32)
    if shards:
        result = result * levels(key, shape, shards, -0.22, 0.18)
    return jnp.clip(strengthened(result, jax.random.fold_in(key, 3), *heavy), -most, most).astype(kind)


def setup_inputs(seed: int = 0) -> dict:
    key_list = jax.random.split(jax.random.key(seed), 8)
    tokens = normal_values(key_list[0], (TOKENS, MODEL_FEATURES), 1.0, 6.0, ((0, 8), (1, 8)))
    token_job_index = draw_token_job_index(jax.random.fold_in(key_list[7], 71), 0)
    gate_up_matrix = normal_values(key_list[2], (2, MODEL_FEATURES, HIDDEN_UNITS), MODEL_FEATURES ** -0.5, 0.09375, ((1, 8), (2, 64)))
    down_matrix = heavy_noise(key_list[3], (HIDDEN_UNITS, MODEL_FEATURES), HIDDEN_UNITS ** -0.5, 0.125, ((0, 64), (1, 8)), (0, 1, 64, 4.0))
    adapter_input_maps = normal_values(key_list[4], (2, MODEL_FEATURES, JOB_COUNT * ADAPTER_RANK), MODEL_FEATURES ** -0.5, 0.09375, ((1, 8),))
    adapter_output_maps = normal_values(key_list[5], (2, JOB_COUNT * ADAPTER_RANK, HIDDEN_UNITS), ADAPTER_RANK ** -0.5, 1.5, ((2, 64),))
    cotangent = normal_values(key_list[6], (TOKENS, MODEL_FEATURES), 1.0, 6.0, ((0, 8), (1, 64)))
    return {"tokens": tokens, "token_job_index": token_job_index, "gate_up_matrix": gate_up_matrix, "down_matrix": down_matrix, "adapter_input_maps": adapter_input_maps, "adapter_output_maps": adapter_output_maps, "cotangent": cotangent}


adapter_scale = 0.5


def reference(tokens, token_job_index, gate_up_matrix, down_matrix, adapter_input_maps, adapter_output_maps, cotangent):
    col_job = jnp.arange(JOB_COUNT * ADAPTER_RANK, dtype=jnp.int32) // ADAPTER_RANK
    job_select_mask = (token_job_index[:, None] == col_job[None, :]).astype(jnp.float32)
    reduced_inner = [(jnp.dot(tokens, adapter_input_maps[contraction_index], preferred_element_type=jnp.float32) * job_select_mask).astype(jnp.bfloat16) for contraction_index in range(2)]
    before_activation = [jnp.dot(tokens, gate_up_matrix[contraction_index], preferred_element_type=jnp.float32) + adapter_scale * jnp.dot(reduced_inner[contraction_index], adapter_output_maps[contraction_index], preferred_element_type=jnp.float32) for contraction_index in range(2)]
    gate_pre = before_activation[0]
    up_pre = before_activation[1]
    sigmoid_gate = jax.nn.sigmoid(gate_pre)
    silu_gate = gate_pre * sigmoid_gate
    hidden_state = (silu_gate * up_pre).astype(jnp.bfloat16)
    mixed = jnp.dot(hidden_state, down_matrix, preferred_element_type=jnp.float32).astype(jnp.bfloat16)
    hidden_grad = jnp.dot(cotangent, down_matrix.T, preferred_element_type=jnp.float32)
    gate_grad = hidden_grad * up_pre * sigmoid_gate * (1.0 + gate_pre * (1.0 - sigmoid_gate))
    up_grad = hidden_grad * silu_gate
    before_activation_gradient = [gate_grad.astype(jnp.bfloat16), up_grad.astype(jnp.bfloat16)]
    backward_inner = [adapter_scale * job_select_mask * jnp.dot(before_activation_gradient[contraction_index], adapter_output_maps[contraction_index].T, preferred_element_type=jnp.float32) for contraction_index in range(2)]
    input_gradient = jnp.dot(before_activation_gradient[0], gate_up_matrix[0].T, preferred_element_type=jnp.float32)
    input_gradient = input_gradient + jnp.dot(before_activation_gradient[1], gate_up_matrix[1].T, preferred_element_type=jnp.float32)
    for contraction_index in range(2):
        input_gradient = input_gradient + jnp.dot(backward_inner[contraction_index], adapter_input_maps[contraction_index].astype(jnp.float32).T, precision=lax.Precision.HIGHEST)
    input_gradient = input_gradient.astype(jnp.bfloat16)
    token_rows_broad = tokens.astype(jnp.float32)
    adapter_input_gradient = jnp.stack([jnp.dot(token_rows_broad.T, backward_inner[contraction_index], precision=lax.Precision.HIGHEST) for contraction_index in range(2)])
    adapter_output_gradient = jnp.stack([adapter_scale * jnp.dot(reduced_inner[contraction_index].T, before_activation_gradient[contraction_index], preferred_element_type=jnp.float32) for contraction_index in range(2)])
    return mixed, input_gradient, adapter_input_gradient, adapter_output_gradient
```

```python
import functools

import jax
import jax.numpy as jnp
from jax import lax
from jax.experimental import pallas as pl
from jax.experimental.pallas import tpu as pltpu
from jax.sharding import PartitionSpec as P

JOB_COUNT = 16
ADAPTER_RANK = 16
JOB_COLS = JOB_COUNT * ADAPTER_RANK
JOB_ROWS = 128
SCALE = 0.5
F32 = jnp.float32
BF16 = jnp.bfloat16

NX, NYLO, NYHI, NCORE, NZ = 4, 2, 4, 2, 8
NY = NYLO * NYHI
PIECE = 64
FEAT = NX * NYLO * PIECE
TOK = NYHI * NCORE * JOB_ROWS
HID = 224
LOW = 2 * ADAPTER_RANK
ROWS = 3 * HID + LOW
HALF = ROWS // 2


def mm(a, b):
    return jnp.dot(a, b, preferred_element_type=F32)


def mm_nt(a, b):
    return lax.dot_general(a, b, (((1,), (1,)), ((), ())), preferred_element_type=F32)


def kernel(
    tok_ref, job_ref, gu_ref, dn_ref, a_ref, b_ref, cot_ref,
    mixed_ref, ig_ref, ga_ref, gb_ref,
    xc, jobs, tok_t, w1t, dnt, at, bt,
    part, send_r, send_l, recv_r, recv_l, held,
    outp, core_in, x_out, x_in, y_out, y_in,
    b_core_out, b_core_in, b_x_out, b_x_in, b_y_out, b_y_in, inner,
    ag_y_s, ag_y_r, job_y_s, job_y_r, ag_x_s, ag_x_r, ag_c_s, ag_c_r,
    rs_s, rs_r, zg_s, zg_r, oc_s, oc_r, ox_s, ox_r, oy_s, oy_r,
    bc_s, bc_r, bx_s, bx_r, by_s, by_r, bz_s, bz_r,
):
    dp = lax.axis_index("dp")
    z = lax.axis_index("width")
    hid = lax.axis_index("hidden")
    yhi, core = dp // NCORE, dp % NCORE
    ylo, x = hid // NX, hid % NX
    y = yhi * NYLO + ylo
    right, left = (z + 1) % NZ, (z + NZ - 1) % NZ
    sibling = (yhi * NCORE + 1 - core, z, hid)

    def y_dev(other):
        return ((other // NYLO) * NCORE + core, z, (other % NYLO) * NX + x)

    def x_dev(other):
        return (dp, z, ylo * NX + other)

    def z_dev(other):
        return (dp, other, hid)

    def send(src, dst, s, r, dev):
        copy = pltpu.make_async_remote_copy(
            src_ref=src, dst_ref=dst, send_sem=s, recv_sem=r,
            device_id=dev, device_id_type=pl.DeviceIdType.MESH,
        )
        copy.start()
        sent.append(copy)

    def arrived(dst, s, r):
        pltpu.make_async_remote_copy(
            src_ref=dst, dst_ref=dst, send_sem=s, recv_sem=r,
            device_id=sibling, device_id_type=pl.DeviceIdType.MESH,
        ).wait_recv()

    sent = []
    barrier = pltpu.get_barrier_semaphore()
    partners = [sibling]
    partners += [y_dev((y + k) % NY) for k in range(1, NY)]
    partners += [x_dev((x + k) % NX) for k in range(1, NX)]
    partners += [z_dev((z + k) % NZ) for k in range(1, NZ)]
    for dev in partners:
        pl.semaphore_signal(barrier, inc=1, device_id=dev, device_id_type=pl.DeviceIdType.MESH)

    own_lanes = pl.ds(pl.multiple_of((core * NYHI + yhi) * JOB_ROWS, JOB_ROWS), JOB_ROWS)
    core_lanes = pl.ds(pl.multiple_of(core * (TOK // 2), TOK // 2), TOK // 2)
    peer_lanes = pl.ds(pl.multiple_of((1 - core) * (TOK // 2), TOK // 2), TOK // 2)
    tok_t[...] = tok_ref[...].T.reshape(NYLO, NX, PIECE, JOB_ROWS)
    xc[0, ylo, x, :, own_lanes] = tok_t[ylo, x]
    xc[1, ylo, x, :, own_lanes] = cot_ref[...].astype(F32).T.astype(BF16)
    jobs[:, own_lanes] = jnp.broadcast_to(job_ref[...].astype(F32), (16, JOB_ROWS)).astype(BF16)
    pl.semaphore_wait(barrier, len(partners))

    def lanes_of(other):
        return pl.ds(pl.multiple_of((core * NYHI + other // NYLO) * JOB_ROWS, JOB_ROWS), JOB_ROWS)

    own_piece = xc.at[:, ylo, x, :, own_lanes]
    own_jobs = jobs.at[:, own_lanes]
    for k in range(1, NY):
        dev = y_dev((y + k) % NY)
        send(own_piece, own_piece, ag_y_s.at[k - 1], ag_y_r.at[k - 1], dev)
    for k in range(1, NYHI):
        dev = y_dev((y + NYLO * k) % NY)
        send(own_jobs, own_jobs, job_y_s.at[k - 1], job_y_r.at[k - 1], dev)
    for k in range(2):
        w1t[k * HID:(k + 1) * HID, :] = gu_ref[k].T
        at[k * JOB_COLS:(k + 1) * JOB_COLS, :] = a_ref[k].T
        bt[k] = b_ref[k].T
    dnt[...] = dn_ref[...].T
    for k in range(1, NY):
        other = (y + NY - k) % NY
        arrived(xc.at[:, other % NYLO, x, :, lanes_of(other)], ag_y_s.at[k - 1], ag_y_r.at[k - 1])
    for k in range(1, NYHI):
        other = (y + NY - NYLO * k) % NY
        arrived(jobs.at[:, lanes_of(other)], job_y_s.at[k - 1], job_y_r.at[k - 1])

    mine = xc.at[:, :, x, :, core_lanes]
    for k in range(1, NX):
        send(mine, mine, ag_x_s.at[k - 1], ag_x_r.at[k - 1], x_dev((x + k) % NX))
    send(jobs.at[:, core_lanes], jobs.at[:, core_lanes], ag_c_s.at[1], ag_c_r.at[1], sibling)
    for k in range(1, NX):
        arrived(xc.at[:, :, (x + NX - k) % NX, :, core_lanes], ag_x_s.at[k - 1], ag_x_r.at[k - 1])
    half = xc.at[:, :, :, :, core_lanes]
    send(half, half, ag_c_s.at[0], ag_c_r.at[0], sibling)
    arrived(jobs.at[:, peer_lanes], ag_c_s.at[1], ag_c_r.at[1])
    arrived(xc.at[:, :, :, :, peer_lanes], ag_c_s.at[0], ag_c_r.at[0])

    def job_mask(lanes, width):
        row = jobs[:, lanes].astype(F32)[0:1]
        col = lax.broadcasted_iota(jnp.int32, (JOB_COLS, width), 0) // ADAPTER_RANK
        return col.astype(F32) == row

    @pl.loop(0, TOK // 256)
    def _(q):
        lanes = pl.ds(pl.multiple_of(q * 256, 256), 256)
        rows = xc[0, :, :, :, lanes].reshape(FEAT, 256)
        grads = xc[1, :, :, :, lanes].reshape(FEAT, 256)
        pre = mm(w1t[...], rows)
        back = mm(dn_ref[...], grads)
        mask = job_mask(lanes, 256)
        low = mm(at[...], rows)
        lows = []
        for k in range(2):
            picked = jnp.where(mask, low[k * JOB_COLS:(k + 1) * JOB_COLS], 0.0)
            lows.append(picked.reshape(JOB_COUNT, ADAPTER_RANK, 256).sum(0))
        for i in range(2):
            cut = slice(i * 128, (i + 1) * 128)
            part[2 * q + i, 0:2 * HID, :] = pre[:, cut]
            part[2 * q + i, 2 * HID:3 * HID, :] = back[:, cut]
            for k in range(2):
                at_row = 3 * HID + k * ADAPTER_RANK
                part[2 * q + i, at_row:at_row + ADAPTER_RANK, :] = lows[k][:, cut]

    first, second = pl.ds(0, HALF), pl.ds(HALF, HALF)
    far = (z + NZ // 2) % NZ
    send_r[0, first, :] = part[far, first, :].astype(BF16)
    send(send_r.at[0, first], recv_r.at[0, first], rs_s.at[0, 0], rs_r.at[0, 0], z_dev(right))
    send_l[0, second, :] = part[far, second, :].astype(BF16)
    send(send_l.at[0, second], recv_l.at[0, second], rs_s.at[1, 0], rs_r.at[1, 0], z_dev(left))
    for t in range(1, 4):
        block_r, block_l = (z + 4 - t) % NZ, (z + 4 + t) % NZ
        if t == 1:
            send_r[t, second, :] = part[block_r, second, :].astype(BF16)
            arrived(recv_r.at[0, first], rs_s.at[0, 0], rs_r.at[0, 0])
            send_r[t, first, :] = (part[block_r, first, :] + recv_r[0, first, :].astype(F32)).astype(BF16)
        else:
            arrived(recv_r.at[t - 1], rs_s.at[0, t - 1], rs_r.at[0, t - 1])
            send_r[t] = (part[block_r] + recv_r[t - 1].astype(F32)).astype(BF16)
        send(send_r.at[t], recv_r.at[t], rs_s.at[0, t], rs_r.at[0, t], z_dev(right))
        if t == 1:
            send_l[t, first, :] = part[block_l, first, :].astype(BF16)
            arrived(recv_l.at[0, second], rs_s.at[1, 0], rs_r.at[1, 0])
            send_l[t, second, :] = (part[block_l, second, :] + recv_l[0, second, :].astype(F32)).astype(BF16)
        else:
            arrived(recv_l.at[t - 1], rs_s.at[1, t - 1], rs_r.at[1, t - 1])
            send_l[t] = (part[block_l] + recv_l[t - 1].astype(F32)).astype(BF16)
        send(send_l.at[t], recv_l.at[t], rs_s.at[1, t], rs_r.at[1, t], z_dev(left))
    arrived(recv_r.at[3], rs_s.at[0, 3], rs_r.at[0, 3])
    arrived(recv_l.at[3], rs_s.at[1, 3], rs_r.at[1, 3])
    total = part[z] + recv_r[3].astype(F32) + recv_l[3].astype(F32)

    mask = job_mask(pl.ds(pl.multiple_of(z * JOB_ROWS, JOB_ROWS), JOB_ROWS), JOB_ROWS)
    pre_act = []
    for k in range(2):
        low = total[3 * HID + k * ADAPTER_RANK:3 * HID + (k + 1) * ADAPTER_RANK]
        wide = jnp.where(mask, jnp.concatenate([low] * JOB_COUNT, axis=0), 0.0).astype(BF16)
        pre_act.append(total[k * HID:(k + 1) * HID] + SCALE * mm(bt[k], wide))
    gate, up = pre_act
    back = total[2 * HID:3 * HID]
    sig = jax.nn.sigmoid(gate)
    silu = gate * sig
    grads = [
        (back * up * sig * (1.0 + gate * (1.0 - sig))).astype(BF16),
        (back * silu).astype(BF16),
    ]
    held[z, 0:HID, :] = (silu * up).astype(BF16)
    held[z, HID:2 * HID, :] = grads[0]
    held[z, 2 * HID:3 * HID, :] = grads[1]
    held[z, 3 * HID:, :] = total[3 * HID:].astype(BF16)
    send(held.at[z], held.at[z], zg_s.at[0, 0], zg_r.at[0, 0], z_dev(right))
    send(held.at[z], held.at[z], zg_s.at[1, 0], zg_r.at[1, 0], z_dev(left))
    for k in range(2):
        wide = jnp.where(mask, mm(b_ref[k], grads[k]), 0.0)
        b_core_out[k * ADAPTER_RANK:(k + 1) * ADAPTER_RANK, :] = SCALE * wide.reshape(
            JOB_COUNT, ADAPTER_RANK, JOB_ROWS
        ).sum(0)
    send(b_core_out, b_core_in, bc_s.at[0], bc_r.at[0], sibling)

    def outputs_of(blocks):
        def rows_of(lo, hi):
            return jnp.concatenate([held[p, lo:hi, :] for p in blocks], axis=1)

        out = mm(dnt[...], rows_of(0, HID))
        grad = mm(gu_ref[0], rows_of(HID, 2 * HID)) + mm(gu_ref[1], rows_of(2 * HID, 3 * HID))
        for i, p in enumerate(blocks):
            cut = slice(i * 128, (i + 1) * 128)
            outp[p, 0] = out[:, cut].astype(BF16).reshape(NYLO, NX, PIECE, JOB_ROWS)
            outp[p, 1] = grad[:, cut].astype(BF16).reshape(NYLO, NX, PIECE, JOB_ROWS)

    outputs_of([z])
    for t in range(1, 4):
        block_r, block_l = (z + NZ - t) % NZ, (z + t) % NZ
        arrived(held.at[block_r], zg_s.at[0, t - 1], zg_r.at[0, t - 1])
        piece = held.at[block_r, first] if t == 3 else held.at[block_r]
        send(piece, piece, zg_s.at[0, t], zg_r.at[0, t], z_dev(right))
        arrived(held.at[block_l], zg_s.at[1, t - 1], zg_r.at[1, t - 1])
        piece = held.at[block_l, second] if t == 3 else held.at[block_l]
        send(piece, piece, zg_s.at[1, t], zg_r.at[1, t], z_dev(left))
        if t == 1:
            arrived(b_core_in, bc_s.at[0], bc_r.at[0])
            b_x_out[...] = b_core_out[...] + b_core_in[...]
            for k in range(1, NX):
                send(b_x_out, b_x_in.at[k - 1], bx_s.at[k - 1], bx_r.at[k - 1], x_dev((x + k) % NX))
        elif t == 2:
            both = b_x_out[...]
            for k in range(1, NX):
                arrived(b_x_in.at[k - 1], bx_s.at[k - 1], bx_r.at[k - 1])
                both = both + b_x_in[k - 1]
            b_y_out[...] = both
            for k in range(1, NY):
                send(b_y_out, b_y_in.at[k - 1], by_s.at[k - 1], by_r.at[k - 1], y_dev((y + k) % NY))
        else:
            both = b_y_out[...]
            for k in range(1, NY):
                arrived(b_y_in.at[k - 1], by_s.at[k - 1], by_r.at[k - 1])
                both = both + b_y_in[k - 1]
            inner[z] = both
            for k in range(1, NZ):
                send(inner.at[z], inner.at[z], bz_s.at[k - 1], bz_r.at[k - 1], z_dev((z + k) % NZ))
        outputs_of([block_r, block_l])
    arrived(held.at[far, first], zg_s.at[0, 3], zg_r.at[0, 3])
    arrived(held.at[far, second], zg_s.at[1, 3], zg_r.at[1, 3])
    outputs_of([far])

    peer_blocks = pl.ds((1 - core) * NYHI, NYHI)
    send(outp.at[peer_blocks], core_in, oc_s.at[0], oc_r.at[0], sibling)
    for k in range(2):
        acc = jnp.zeros((JOB_COLS, HID), F32)
        for q in range(TOK // 256):
            at_row = 3 * HID + k * ADAPTER_RANK
            low = jnp.concatenate(
                [held[2 * q + i, at_row:at_row + ADAPTER_RANK, :] for i in range(2)], axis=1
            ).astype(F32)
            wide = jnp.where(
                job_mask(pl.ds(q * 256, 256), 256), jnp.concatenate([low] * JOB_COUNT, axis=0), 0.0
            ).astype(BF16)
            grad = jnp.concatenate(
                [held[2 * q + i, (1 + k) * HID:(2 + k) * HID, :] for i in range(2)], axis=1
            )
            acc = acc + mm_nt(wide, grad)
        gb_ref[k] = SCALE * acc
    arrived(core_in, oc_s.at[0], oc_r.at[0])
    for i in range(NYHI):
        x_out[i] = (outp[core * NYHI + i].astype(F32) + core_in[i].astype(F32)).astype(BF16)
    for k in range(1, NX):
        other = (x + k) % NX
        send(x_out.at[:, :, :, other], x_in.at[k - 1], ox_s.at[k - 1], ox_r.at[k - 1], x_dev(other))
    for k in range(1, NZ):
        arrived(inner.at[(z + NZ - k) % NZ], bz_s.at[k - 1], bz_r.at[k - 1])

    def wide_inner(k, p, mask):
        part_inner = inner[p, k * ADAPTER_RANK:(k + 1) * ADAPTER_RANK, :]
        wide = jnp.where(mask, jnp.concatenate([part_inner] * JOB_COUNT, axis=0), 0.0)
        hi = wide.astype(BF16)
        return hi, (wide - hi.astype(F32)).astype(BF16)

    for k in range(2):
        acc = jnp.zeros((FEAT, JOB_COLS), F32)
        for q in range(TOK // 256):
            rows = xc[0, :, :, :, q * 256:(q + 1) * 256].reshape(FEAT, 256)
            parts = []
            for p in (2 * q, 2 * q + 1):
                parts.append(wide_inner(k, p, job_mask(pl.ds(p * 128, 128), 128)))
            acc = acc + mm_nt(rows, jnp.concatenate([parts[0][0], parts[1][0]], axis=1))
            acc = acc + mm_nt(rows, jnp.concatenate([parts[0][1], parts[1][1]], axis=1))
        ga_ref[k] = acc
    for k in range(1, NX):
        arrived(x_in.at[k - 1], ox_s.at[k - 1], ox_r.at[k - 1])
    for i in range(NYHI):
        both = x_out[i, :, :, x].astype(F32)
        for k in range(1, NX):
            both = both + x_in[k - 1, i].astype(F32)
        y_out[i] = both.astype(BF16)
    for k in range(1, NY):
        other = (y + k) % NY
        send(y_out.at[other // NYLO, :, other % NYLO], y_in.at[k - 1],
             oy_s.at[k - 1], oy_r.at[k - 1], y_dev(other))
    own_block = core * NYHI + yhi
    mask = job_mask(own_lanes, JOB_ROWS)
    extra = jnp.zeros((PIECE, JOB_ROWS), F32)
    for k in range(2):
        cols = a_ref[k, pl.ds(pl.multiple_of(hid * PIECE, PIECE), PIECE), :]
        for wide in wide_inner(k, own_block, mask):
            extra = extra + mm(cols, wide)
    out = y_out[yhi, 0, ylo].astype(F32)
    grad = y_out[yhi, 1, ylo].astype(F32) + extra
    for k in range(1, NY):
        arrived(y_in.at[k - 1], oy_s.at[k - 1], oy_r.at[k - 1])
        out = out + y_in[k - 1, 0].astype(F32)
        grad = grad + y_in[k - 1, 1].astype(F32)
    mixed_ref[...] = out.T.astype(BF16)
    ig_ref[...] = grad.T.astype(BF16)
    for copy in sent:
        copy.wait_send()


def local(tokens, token_job_index, gate_up, down, adapter_in, adapter_out, cotangent):
    vmem = pl.BlockSpec(memory_space=pltpu.VMEM)
    dma = lambda *shape: pltpu.SemaphoreType.DMA(shape)
    buf = pltpu.VMEM
    tile = (PIECE, JOB_ROWS)
    sems = [
        NY - 1, NY - 1, NYHI - 1, NYHI - 1, NX - 1, NX - 1, 2, 2,
        (2, 4), (2, 4), (2, 4), (2, 4), 1, 1, NX - 1, NX - 1, NY - 1, NY - 1,
        1, 1, NX - 1, NX - 1, NY - 1, NY - 1, NZ - 1, NZ - 1,
    ]
    return pl.pallas_call(
        kernel,
        out_shape=[
            jax.ShapeDtypeStruct((JOB_ROWS, PIECE), BF16),
            jax.ShapeDtypeStruct((JOB_ROWS, PIECE), BF16),
            jax.ShapeDtypeStruct((2, FEAT, JOB_COLS), F32),
            jax.ShapeDtypeStruct((2, JOB_COLS, HID), F32),
        ],
        in_specs=[vmem] * 7,
        out_specs=[vmem] * 4,
        scratch_shapes=[
            buf((2, NYLO, NX, PIECE, TOK), BF16),
            buf((16, TOK), BF16),
            buf((NYLO, NX) + tile, BF16),
            buf((2 * HID, FEAT), BF16),
            buf((FEAT, HID), BF16),
            buf((2 * JOB_COLS, FEAT), BF16),
            buf((2, HID, JOB_COLS), BF16),
            buf((NZ, ROWS, JOB_ROWS), F32),
            buf((4, ROWS, JOB_ROWS), BF16),
            buf((4, ROWS, JOB_ROWS), BF16),
            buf((4, ROWS, JOB_ROWS), BF16),
            buf((4, ROWS, JOB_ROWS), BF16),
            buf((NZ, ROWS, JOB_ROWS), BF16),
            buf((NZ, 2, NYLO, NX) + tile, BF16),
            buf((NYHI, 2, NYLO, NX) + tile, BF16),
            buf((NYHI, 2, NYLO, NX) + tile, BF16),
            buf((NX - 1, NYHI, 2, NYLO) + tile, BF16),
            buf((NYHI, 2, NYLO) + tile, BF16),
            buf((NY - 1, 2) + tile, BF16),
            buf((LOW, JOB_ROWS), F32),
            buf((LOW, JOB_ROWS), F32),
            buf((LOW, JOB_ROWS), F32),
            buf((NX - 1, LOW, JOB_ROWS), F32),
            buf((LOW, JOB_ROWS), F32),
            buf((NY - 1, LOW, JOB_ROWS), F32),
            buf((NZ, LOW, JOB_ROWS), F32),
        ] + [dma(*s) if isinstance(s, tuple) else dma(s) for s in sems],
        compiler_params=pltpu.CompilerParams(
            collective_id=0, has_side_effects=True, vmem_limit_bytes=44 * 1024 * 1024
        ),
    )(
        tokens, token_job_index.reshape(1, JOB_ROWS), gate_up, down,
        adapter_in, adapter_out, cotangent,
    )


def solution(mesh):
    return jax.shard_map(
        local,
        mesh=mesh,
        in_specs=(
            P("dp", "width"),
            P("dp"),
            P(None, "width", ("dp", "hidden")),
            P(("dp", "hidden"), "width"),
            P(None, "width", None),
            P(None, None, ("dp", "hidden")),
            P("dp", ("width", "hidden")),
        ),
        out_specs=(
            P("dp", ("width", "hidden")),
            P("dp", ("width", "hidden")),
            P(None, "width", None),
            P(None, None, ("dp", "hidden")),
        ),
        check_vma=False,
    )
```

```python
import jax
import jax.numpy as jnp
from jax import lax
from jax.experimental import pallas as pl
from jax.experimental.pallas import tpu as pltpu
from jax.sharding import PartitionSpec as P

JOB_COUNT = 16
ADAPTER_RANK = 16
JOB_COLS = JOB_COUNT * ADAPTER_RANK
JOB_ROWS = 128
SCALE = 0.5
F32 = jnp.float32
BF16 = jnp.bfloat16

NX, NYLO, NYHI, NCORE, NZ = 4, 2, 4, 2, 8
NY = NYLO * NYHI
PIECE = 64
FEAT = NX * NYLO * PIECE
HID = 224
LOW = 2 * ADAPTER_RANK
SUMS = ((0, 240), (240, 480), (480, 592), (592, 704))
LOW_AT, BACK_AT = 2 * HID, 2 * HID + LOW
PARTS = ((0, 128), (128, 256), (256, 480), (480, 704))
HLOW_AT, GRAD_AT = HID, HID + LOW
ROWS = 3 * HID + LOW


def mm(a, b):
    return jnp.dot(a, b, preferred_element_type=F32)


def mm_nt(a, b):
    return lax.dot_general(a, b, (((1,), (1,)), ((), ())), preferred_element_type=F32)


def kernel(
    tok_hbm, job_hbm, gut_hbm, dn_hbm, a_hbm, bt_hbm, cot_hbm,
    mixed_hbm, ig_hbm, ga_hbm, gb_hbm,
    tok_ref, job_ref, gut_ref, dn_ref, a_ref, bt_ref,
    mixed_ref, ig_ref, ga_ref, gb_ref,
    xc, jobs, gu, dnt, at, bn,
    part, ring_out, ring_in, held,
    outp, core_in, x_out, x_in, y_out, y_in, fin, fin_in,
    b_core_out, b_core_in, b_x_out, b_x_in, b_y_out, b_y_in, inner,
    ty_s, ty_r, tx_s, tx_r, tf_s, tf_r, tc_s, tc_r, jy_s, jy_r, jc_s, jc_r,
    rs_s, rs_r, zg_s, zg_r, oc_s, oc_r, ox_s, ox_r, oy_s, oy_r, of_s, of_r,
    bc_s, bc_r, bx_s, bx_r, by_s, by_r, bz_s, bz_r, load_s, store_s,
):
    dp = lax.axis_index("dp")
    z = lax.axis_index("width")
    hid = lax.axis_index("hidden")
    yhi, core = dp // NCORE, dp % NCORE
    ylo, x = hid // NX, hid % NX
    y = yhi * NYLO + ylo
    sibling = (yhi * NCORE + 1 - core, z, hid)
    far = (z + NZ // 2) % NZ

    def y_dev(other):
        return ((other // NYLO) * NCORE + core, z, (other % NYLO) * NX + x)

    def x_dev(other):
        return (dp, z, ylo * NX + other)

    def z_dev(other):
        return (dp, other, hid)

    next_dev = (z_dev((z + 1) % NZ), z_dev((z + NZ - 1) % NZ))
    sent = []

    def send(src, dst, s, r, dev):
        copy = pltpu.make_async_remote_copy(
            src_ref=src, dst_ref=dst, send_sem=s, recv_sem=r,
            device_id=dev, device_id_type=pl.DeviceIdType.MESH,
        )
        copy.start()
        sent.append(copy)

    def arrived(dst, s, r):
        pltpu.make_async_remote_copy(
            src_ref=dst, dst_ref=dst, send_sem=s, recv_sem=r,
            device_id=sibling, device_id_type=pl.DeviceIdType.MESH,
        ).wait_recv()

    own_cot = xc.at[yhi, core, ylo, x, 1]
    loads = {}
    for i, (src, dst) in enumerate((
        (tok_hbm, tok_ref), (cot_hbm, own_cot), (job_hbm, job_ref), (a_hbm, a_ref),
        (gut_hbm, gut_ref), (dn_hbm, dn_ref), (bt_hbm, bt_ref),
    )):
        loads[i] = pltpu.make_async_copy(src, dst, load_s.at[i])
        loads[i].start()
    stores = []

    def store(i, src, dst):
        copy = pltpu.make_async_copy(src, dst, store_s.at[i])
        copy.start()
        stores.append(copy)

    barrier = pltpu.get_barrier_semaphore()
    partners = [sibling]
    partners += [y_dev((y + k) % NY) for k in range(1, NY)]
    partners += [x_dev((x + k) % NX) for k in range(1, NX)]
    partners += [z_dev((z + k) % NZ) for k in range(1, NZ)]
    for dev in partners:
        pl.semaphore_signal(barrier, inc=1, device_id=dev, device_id_type=pl.DeviceIdType.MESH)
    eye = (
        lax.broadcasted_iota(jnp.int32, (256, 256), 0)
        == lax.broadcasted_iota(jnp.int32, (256, 256), 1)
    ).astype(F32).astype(BF16)

    def turned(ref):
        cols = ref.shape[1]
        return jnp.concatenate(
            [mm_nt(eye, ref[:, i:i + 256]) for i in range(0, cols, 256)], axis=0
        ).astype(BF16)

    loads[0].wait()
    xc[yhi, core, :, :, 0] = turned(tok_ref).reshape(NYLO, NX, PIECE, JOB_ROWS)
    loads[1].wait()
    loads[2].wait()
    jobs[yhi, core] = jnp.broadcast_to(job_ref[...].astype(F32), (16, JOB_ROWS)).astype(BF16)
    pl.semaphore_wait(barrier, len(partners))

    def piece(k, src, low, at_x):
        view = xc.at[src, core, low, at_x]
        return view if k else xc.at[src, core, low, at_x, 1]

    both_low = pl.ds(0, NYLO)
    order = (0, 1, 3, 2)
    source = [(yhi + NYHI - k) % NYHI for k in range(NYHI)]
    own = xc.at[yhi, core, ylo, x]
    send(own_cot, own_cot, ty_s.at[0, 0], ty_r.at[0, 0], y_dev(yhi * NYLO + 1 - ylo))
    for k in order[1:]:
        for low in range(NYLO):
            dev = y_dev(((yhi + k) % NYHI) * NYLO + low)
            send(own, own, ty_s.at[k, low], ty_r.at[k, ylo], dev)
    own = xc.at[yhi, core, :, :, 0]
    send(own, own, tc_s.at[NYHI], tc_r.at[NYHI], sibling)
    own = jobs.at[yhi, core]
    for k in range(1, NYHI):
        dev = y_dev(((yhi + k) % NYHI) * NYLO + ylo)
        send(own, own, jy_s.at[k - 1], jy_r.at[k - 1], dev)
    loads[3].wait()
    for k in range(2):
        at[k * JOB_COLS:(k + 1) * JOB_COLS, :] = turned(a_ref.at[k])
    x_next = (x_dev((x + 1) % NX), x_dev((x + NX - 1) % NX))
    x_from = ((x + NX - 1) % NX, (x + 1) % NX)
    for k in order:
        src = source[k]
        if k == 0:
            arrived(piece(0, src, 1 - ylo, x), ty_s.at[0, 0], ty_r.at[0, 0])
        else:
            for low in range(NYLO):
                arrived(piece(k, src, low, x), ty_s.at[k, low], ty_r.at[k, low])
        for way in range(2):
            own = piece(k, src, both_low, x)
            send(own, own, tx_s.at[k, way], tx_r.at[k, way], x_next[way])
    for k in range(1, NYHI):
        arrived(jobs.at[source[k], core], jy_s.at[k - 1], jy_r.at[k - 1])
    send(jobs.at[:, core], jobs.at[:, core], jc_s.at[0], jc_r.at[0], sibling)
    for i in range(4, 7):
        loads[i].wait()
    for k in range(2):
        gu[k] = turned(gut_ref.at[k])
        bn[k] = turned(bt_ref.at[k])
    dnt[...] = turned(dn_ref)
    for k in order:
        for way in range(2):
            arrived(piece(k, source[k], both_low, x_from[way]), tx_s.at[k, way], tx_r.at[k, way])
            onward = piece(k, source[k], way, x_from[way])
            send(onward, onward, tf_s.at[k, way], tf_r.at[k, way], x_next[way])
    for k in order:
        for way in range(2):
            across = piece(k, source[k], way, (x + 2) % NX)
            arrived(across, tf_s.at[k, way], tf_r.at[k, way])
        whole = xc.at[source[k], core] if k else xc.at[yhi, core, :, :, 1]
        send(whole, whole, tc_s.at[k], tc_r.at[k], sibling)
    arrived(jobs.at[:, 1 - core], jc_s.at[0], jc_r.at[0])
    arrived(xc.at[yhi, 1 - core, :, :, 0], tc_s.at[NYHI], tc_r.at[NYHI])
    for k in order:
        whole = xc.at[source[k], 1 - core] if k else xc.at[yhi, 1 - core, :, :, 1]
        arrived(whole, tc_s.at[k], tc_r.at[k])

    def wide_mask(row):
        row = row.astype(F32)[0:1]
        col = lax.broadcasted_iota(jnp.int32, (JOB_COLS, row.shape[1]), 0) // ADAPTER_RANK
        return col.astype(F32) == row

    def pair(kind, q):
        return jnp.concatenate(
            [xc[q, c, :, :, kind].reshape(FEAT, JOB_ROWS) for c in range(NCORE)], axis=1
        )

    def pair_mask(q):
        return wide_mask(jnp.concatenate([jobs[q, c] for c in range(NCORE)], axis=1))

    def forward_sums(q):
        rows = pair(0, q)
        mask = pair_mask(q)
        pre = [mm(gut_ref[k], rows) for k in range(2)]
        low = mm(at[...], rows)
        for k in range(2):
            picked = jnp.where(mask, low[k * JOB_COLS:(k + 1) * JOB_COLS], 0.0)
            picked = picked.reshape(JOB_COUNT, ADAPTER_RANK, 2 * JOB_ROWS).sum(0)
            low_at = LOW_AT + k * ADAPTER_RANK
            for c in range(NCORE):
                cut = slice(c * JOB_ROWS, (c + 1) * JOB_ROWS)
                part[NCORE * q + c, k * HID:(k + 1) * HID, :] = pre[k][:, cut]
                part[NCORE * q + c, low_at:low_at + ADAPTER_RANK, :] = picked[:, cut]

    def backward_sums(q):
        back = mm(dn_ref[...], pair(1, q))
        for c in range(NCORE):
            part[NCORE * q + c, BACK_AT:, :] = back[:, c * JOB_ROWS:(c + 1) * JOB_ROWS]

    def sum_step(t, chunks):
        ready = []
        for way in range(2):
            cuts = [c for c in chunks if t > 0 or c % 2 == way]
            cuts.sort(key=lambda c: c % 2 == way)
            ready.append(cuts)
        for cuts in zip(*ready):
            for way, c in enumerate(cuts):
                block = (z + 4 - t) % NZ if way == 0 else (z + 4 + t) % NZ
                lo, hi = SUMS[c]
                value = part[block, lo:hi, :]
                if t > 1 or (t == 1 and c % 2 == way):
                    before = ring_in.at[way, t - 1, lo:hi]
                    arrived(before, rs_s.at[way, t - 1, c], rs_r.at[way, t - 1, c])
                    value = value + before[...].astype(F32)
                ring_out[way, t, lo:hi, :] = value.astype(BF16)
                send(ring_out.at[way, t, lo:hi], ring_in.at[way, t, lo:hi],
                     rs_s.at[way, t, c], rs_r.at[way, t, c], next_dev[way])

    def sum_end(chunks):
        for c in chunks:
            lo, hi = SUMS[c]
            for way in range(2):
                arrived(ring_in.at[way, 3, lo:hi], rs_s.at[way, 3, c], rs_r.at[way, 3, c])
        lo, hi = SUMS[chunks[0]][0], SUMS[chunks[-1]][1]
        return part[z, lo:hi, :] + (
            ring_in[0, 3, lo:hi, :].astype(F32) + ring_in[1, 3, lo:hi, :].astype(F32)
        )

    def gather_step(t, chunks):
        for c in chunks:
            lo, hi = PARTS[c]
            for way in range(2):
                block = (z + NZ - t) % NZ if way == 0 else (z + t) % NZ
                piece = held.at[block, lo:hi]
                if t > 0:
                    arrived(piece, zg_s.at[way, t - 1, c], zg_r.at[way, t - 1, c])
                if t < 3 or c % 2 == way:
                    send(piece, piece, zg_s.at[way, t, c], zg_r.at[way, t, c], next_dev[way])

    def gather_end(chunks):
        for c in chunks:
            lo, hi = PARTS[c]
            arrived(held.at[far, lo:hi], zg_s.at[c % 2, 3, c], zg_r.at[c % 2, 3, c])

    def blocks_at(t):
        if t == 0 or t == 4:
            return [(z + t) % NZ]
        return [(z + NZ - t) % NZ, (z + t) % NZ]

    def held_rows(blocks, lo, hi):
        return jnp.concatenate([held[p, lo:hi, :] for p in blocks], axis=1)

    def slots(t):
        first = (0, 1, 3, 5, 7)[t]
        return [(first + i, p) for i, p in enumerate(blocks_at(t))]

    def core_stage(t):
        blocks = blocks_at(t)
        values = (
            mm(dnt[...], held_rows(blocks, 0, HID)),
            mm(gu[0], held_rows(blocks, GRAD_AT, GRAD_AT + HID))
            + mm(gu[1], held_rows(blocks, GRAD_AT + HID, ROWS)),
        )
        for j, (n, _) in enumerate(slots(t)):
            for i in range(2):
                cut = values[i][:, j * JOB_ROWS:(j + 1) * JOB_ROWS].astype(BF16)
                outp[n, i] = cut.reshape(NYLO, NX, PIECE, JOB_ROWS)
            send(outp.at[n, 1 - core], core_in.at[n], oc_s.at[n], oc_r.at[n], sibling)

    def x_stage(t):
        for n, _ in slots(t):
            arrived(core_in.at[n], oc_s.at[n], oc_r.at[n])
            x_out[n] = (outp[n, core].astype(F32) + core_in[n].astype(F32)).astype(BF16)
            for k in range(1, NX):
                other = (x + k) % NX
                send(x_out.at[n, :, other], x_in.at[n, k - 1],
                     ox_s.at[n, k - 1], ox_r.at[n, k - 1], x_dev(other))

    def y_copies(n, p):
        for low in range(NYLO):
            other = (p // NCORE) * NYLO + low
            k = (other + NY - y) % NY
            slot = (k + NY - 1) % NY
            yield k, pltpu.make_async_remote_copy(
                src_ref=y_out.at[n, low], dst_ref=y_in.at[p % NCORE, slot],
                send_sem=oy_s.at[n, low], recv_sem=oy_r.at[p % NCORE, slot],
                device_id=y_dev(other), device_id_type=pl.DeviceIdType.MESH,
            )

    def y_stage(t):
        for n, p in slots(t):
            both = x_out[n, :, x].astype(F32)
            for k in range(1, NX):
                arrived(x_in.at[n, k - 1], ox_s.at[n, k - 1], ox_r.at[n, k - 1])
                both = both + x_in[n, k - 1].astype(F32)
            y_out[n] = both.astype(BF16)
            for k, copy in y_copies(n, p):
                @pl.when(k != 0)
                def _(copy=copy):
                    copy.start()

            @pl.when(p // NCORE == yhi)
            def _(n=n, p=p):
                fin[p % NCORE] = y_out[n, ylo].astype(F32)

    forward, backward = (0, 1), (2, 3)
    every = forward + backward
    forward_sums(far // NCORE)
    backward_sums(far // NCORE)
    sum_step(0, every)

    @pl.loop(1, NYHI)
    def _(q):
        forward_sums((far // NCORE + q) % NYHI)
        backward_sums((far // NCORE + q) % NYHI)

    for t in range(1, 4):
        sum_step(t, every)

    total = sum_end(forward)
    mask = wide_mask(jobs[z // NCORE, z % NCORE])
    pre_act = []
    for k in range(2):
        low = total[LOW_AT + k * ADAPTER_RANK:LOW_AT + (k + 1) * ADAPTER_RANK]
        wide = jnp.where(mask, jnp.concatenate([low] * JOB_COUNT, axis=0), 0.0).astype(BF16)
        pre_act.append(total[k * HID:(k + 1) * HID] + SCALE * mm(bt_ref[k], wide))
    gate, up = pre_act
    sig = jax.nn.sigmoid(gate)
    silu = gate * sig
    held[z, 0:HID, :] = (silu * up).astype(BF16)
    held[z, HLOW_AT:GRAD_AT, :] = total[LOW_AT:BACK_AT].astype(BF16)
    gather_step(0, forward)
    back = sum_end(backward)
    grads = [
        (back * up * sig * (1.0 + gate * (1.0 - sig))).astype(BF16),
        (back * silu).astype(BF16),
    ]
    for k in range(2):
        held[z, GRAD_AT + k * HID:GRAD_AT + (k + 1) * HID, :] = grads[k]
    gather_step(0, backward)
    for k in range(2):
        wide = jnp.where(mask, mm(bn[k], grads[k]), 0.0)
        b_core_out[k * ADAPTER_RANK:(k + 1) * ADAPTER_RANK, :] = SCALE * wide.reshape(
            JOB_COUNT, ADAPTER_RANK, JOB_ROWS
        ).sum(0)
    send(b_core_out, b_core_in, bc_s.at[0], bc_r.at[0], sibling)
    core_stage(0)
    gather_step(1, every)
    core_stage(1)
    arrived(b_core_in, bc_s.at[0], bc_r.at[0])
    b_x_out[...] = b_core_out[...] + b_core_in[...]
    for k in range(1, NX):
        send(b_x_out, b_x_in.at[k - 1], bx_s.at[k - 1], bx_r.at[k - 1], x_dev((x + k) % NX))
    x_stage(0)
    gather_step(2, every)
    core_stage(2)
    both = b_x_out[...]
    for k in range(1, NX):
        arrived(b_x_in.at[k - 1], bx_s.at[k - 1], bx_r.at[k - 1])
        both = both + b_x_in[k - 1]
    b_y_out[...] = both
    for k in range(1, NY):
        send(b_y_out, b_y_in.at[k - 1], by_s.at[k - 1], by_r.at[k - 1], y_dev((y + k) % NY))
    x_stage(1)
    y_stage(0)
    gather_step(3, every)
    core_stage(3)
    both = b_y_out[...]
    for k in range(1, NY):
        arrived(b_y_in.at[k - 1], by_s.at[k - 1], by_r.at[k - 1])
        both = both + b_y_in[k - 1]
    inner[z] = both
    for k in range(1, NZ):
        send(inner.at[z], inner.at[z], bz_s.at[k - 1], bz_r.at[k - 1], z_dev((z + k) % NZ))
    x_stage(2)
    y_stage(1)
    gather_end(every)
    core_stage(4)
    x_stage(3)
    y_stage(2)

    for k in range(2):
        acc = jnp.zeros((HID, JOB_COLS), F32)
        for q in range(NYHI):
            blocks = [NCORE * q + c for c in range(NCORE)]
            low_at, grad_at = HLOW_AT + k * ADAPTER_RANK, GRAD_AT + k * HID
            low = held_rows(blocks, low_at, low_at + ADAPTER_RANK).astype(F32)
            wide = jnp.where(pair_mask(q), jnp.concatenate([low] * JOB_COUNT, axis=0), 0.0)
            acc = acc + mm_nt(held_rows(blocks, grad_at, grad_at + HID), wide.astype(BF16))
        gb_ref[k] = SCALE * acc
    store(3, gb_ref, gb_hbm)
    x_stage(4)
    y_stage(3)
    for k in range(1, NZ):
        arrived(inner.at[(z + NZ - k) % NZ], bz_s.at[k - 1], bz_r.at[k - 1])

    def wide_inner(k, blocks, mask):
        rows = [inner[p, k * ADAPTER_RANK:(k + 1) * ADAPTER_RANK, :] for p in blocks]
        rows = jnp.concatenate(rows, axis=1)
        wide = jnp.where(mask, jnp.concatenate([rows] * JOB_COUNT, axis=0), 0.0)
        hi = wide.astype(BF16)
        return hi, (wide - hi.astype(F32)).astype(BF16)

    for k in range(2):
        acc = jnp.zeros((FEAT, JOB_COLS), F32)
        for q in range(NYHI):
            rows = pair(0, q)
            for wide in wide_inner(k, [NCORE * q + c for c in range(NCORE)], pair_mask(q)):
                acc = acc + mm_nt(rows, wide)
        ga_ref[k] = acc
    store(2, ga_ref, ga_hbm)
    y_stage(4)
    mask = wide_mask(jobs[yhi, core])
    extra = jnp.zeros((PIECE, JOB_ROWS), F32)
    for k in range(2):
        cols = a_ref[k, pl.ds(pl.multiple_of(hid * PIECE, PIECE), PIECE), :]
        for wide in wide_inner(k, [dp], mask):
            extra = extra + mm(cols, wide)
    for c in range(NCORE):
        both = fin[c]
        for k in range(1, NY):
            arrived(y_in.at[c, k - 1], oy_s.at[0, 0], oy_r.at[c, k - 1])
            both = both + y_in[c, k - 1].astype(F32)
        fin[c] = both
    send(fin.at[1 - core], fin_in, of_s.at[0], of_r.at[0], sibling)
    arrived(fin_in, of_s.at[0], of_r.at[0])
    mixed_ref[...] = jnp.where(core == 0, fin[0], fin_in[...]).astype(BF16)
    ig_ref[...] = (jnp.where(core == 0, fin_in[...], fin[1]) + extra).astype(BF16)
    store(0, mixed_ref, mixed_hbm)
    store(1, ig_ref, ig_hbm)
    for t in range(5):
        for n, p in slots(t):
            for k, copy in y_copies(n, p):
                @pl.when(k != 0)
                def _(copy=copy):
                    copy.wait_send()
    for copy in stores:
        copy.wait()
    for copy in sent:
        copy.wait_send()


def local(tokens, token_job_index, gate_up, down, adapter_in, adapter_out, cotangent):
    hbm = pl.BlockSpec(memory_space=pltpu.HBM)
    buf = pltpu.VMEM
    tile = (PIECE, JOB_ROWS)
    ring = (2, 4, 4)
    sems = [
        (NYHI, NYLO), (NYHI, 2), (NYHI, 2), (NYHI + 1,), (NYHI - 1,), (1,),
        ring, ring, (NZ,), (NZ, NX - 1), None, (1,),
        (1,), (NX - 1,), (NY - 1,), (NZ - 1,),
    ]
    sems = [(s, s) if s else ((NZ, NYLO), (NCORE, NY - 1)) for s in sems]
    mixed, grad, grad_in, grad_out = pl.pallas_call(
        kernel,
        out_shape=[
            jax.ShapeDtypeStruct(tile, BF16),
            jax.ShapeDtypeStruct(tile, BF16),
            jax.ShapeDtypeStruct((2, FEAT, JOB_COLS), F32),
            jax.ShapeDtypeStruct((2, HID, JOB_COLS), F32),
        ],
        in_specs=[hbm] * 7,
        out_specs=[hbm] * 4,
        scratch_shapes=[
            buf((JOB_ROWS, FEAT), BF16),
            buf((1, JOB_ROWS), jnp.int32),
            buf((2, HID, FEAT), BF16),
            buf((HID, FEAT), BF16),
            buf((2, FEAT, JOB_COLS), BF16),
            buf((2, HID, JOB_COLS), BF16),
            buf(tile, BF16),
            buf(tile, BF16),
            buf((2, FEAT, JOB_COLS), F32),
            buf((2, HID, JOB_COLS), F32),
            buf((NYHI, NCORE, NYLO, NX, 2) + tile, BF16),
            buf((NYHI, NCORE, 16, JOB_ROWS), BF16),
            buf((2, FEAT, HID), BF16),
            buf((FEAT, HID), BF16),
            buf((2 * JOB_COLS, FEAT), BF16),
            buf((2, JOB_COLS, HID), BF16),
            buf((NZ, ROWS, JOB_ROWS), F32),
            buf((2, 4, ROWS, JOB_ROWS), BF16),
            buf((2, 4, ROWS, JOB_ROWS), BF16),
            buf((NZ, ROWS, JOB_ROWS), BF16),
            buf((NZ, 2, NYLO, NX) + tile, BF16),
            buf((NZ, NYLO, NX) + tile, BF16),
            buf((NZ, NYLO, NX) + tile, BF16),
            buf((NZ, NX - 1, NYLO) + tile, BF16),
            buf((NZ, NYLO) + tile, BF16),
            buf((NCORE, NY - 1) + tile, BF16),
            buf((NCORE,) + tile, F32),
            buf(tile, F32),
            buf((LOW, JOB_ROWS), F32),
            buf((LOW, JOB_ROWS), F32),
            buf((LOW, JOB_ROWS), F32),
            buf((NX - 1, LOW, JOB_ROWS), F32),
            buf((LOW, JOB_ROWS), F32),
            buf((NY - 1, LOW, JOB_ROWS), F32),
            buf((NZ, LOW, JOB_ROWS), F32),
        ] + [pltpu.SemaphoreType.DMA(s) for pair in sems for s in pair] + [
            pltpu.SemaphoreType.DMA((7,)), pltpu.SemaphoreType.DMA((4,)),
        ],
        compiler_params=pltpu.CompilerParams(
            collective_id=0, has_side_effects=True, vmem_limit_bytes=63 * 1024 * 1024
        ),
    )(
        tokens, token_job_index.reshape(1, JOB_ROWS), jnp.swapaxes(gate_up, 1, 2), down,
        adapter_in, jnp.swapaxes(adapter_out, 1, 2), cotangent.T,
    )
    return mixed.T, grad.T, grad_in, jnp.swapaxes(grad_out, 1, 2)


def solution(mesh):
    return jax.shard_map(
        local,
        mesh=mesh,
        in_specs=(
            P("dp", "width"),
            P("dp"),
            P(None, "width", ("dp", "hidden")),
            P(("dp", "hidden"), "width"),
            P(None, "width", None),
            P(None, None, ("dp", "hidden")),
            P("dp", ("width", "hidden")),
        ),
        out_specs=(
            P("dp", ("width", "hidden")),
            P("dp", ("width", "hidden")),
            P(None, "width", None),
            P(None, None, ("dp", "hidden")),
        ),
        check_vma=False,
    )
```

```python
import jax
import jax.numpy as jnp
from jax import lax
from jax.experimental import pallas as pl
from jax.experimental.pallas import tpu as pltpu
from jax.sharding import PartitionSpec as P

JOB_COUNT = 16
ADAPTER_RANK = 16
JOB_COLS = JOB_COUNT * ADAPTER_RANK
JOB_ROWS = 128
SCALE = 0.5
F32 = jnp.float32
BF16 = jnp.bfloat16

NX, NYLO, NYHI, NCORE, NZ = 4, 2, 4, 2, 8
NY = NYLO * NYHI
PIECE = 64
FEAT = NX * NYLO * PIECE
HID = 224
LOW = 2 * ADAPTER_RANK
SUMS = ((0, 240), (240, 480), (480, 592), (592, 704))
LOW_AT, BACK_AT = 2 * HID, 2 * HID + LOW
PARTS = ((0, 128), (128, 256), (256, 480), (480, 704))
HLOW_AT, GRAD_AT = HID, HID + LOW
ROWS = 3 * HID + LOW


def mm(a, b):
    return jnp.dot(a, b, preferred_element_type=F32)


def mm_nt(a, b):
    return lax.dot_general(a, b, (((1,), (1,)), ((), ())), preferred_element_type=F32)


def kernel(
    tok_hbm, job_hbm, gut_hbm, dn_hbm, a_hbm, bt_hbm, cot_hbm,
    mixed_hbm, ig_hbm, ga_hbm, gb_hbm,
    tok_ref, job_ref, gut_ref, dn_ref, a_ref, bt_ref,
    mixed_ref, ig_ref, ga_ref, gb_ref,
    xc, jobs, gu, dnt, at, bn,
    part, ring_out, ring_in, held,
    outp, core_in, x_out, x_in, y_out, y_in, fin,
    b_core_out, b_core_in, b_x_out, b_x_in, b_y_out, b_y_in, inner,
    ty_s, ty_r, tx_s, tx_r, tf_s, tf_r, tc_s, tc_r, jy_s, jy_r, jc_s, jc_r,
    rs_s, rs_r, zg_s, zg_r, oc_s, oc_r, ox_s, ox_r, oy_s, oy_r,
    bc_s, bc_r, bx_s, bx_r, by_s, by_r, bz_s, bz_r, load_s, store_s,
):
    dp = lax.axis_index("dp")
    z = lax.axis_index("width")
    hid = lax.axis_index("hidden")
    yhi, core = dp // NCORE, dp % NCORE
    ylo, x = hid // NX, hid % NX
    y = yhi * NYLO + ylo
    sibling = (yhi * NCORE + 1 - core, z, hid)
    far = (z + NZ // 2) % NZ

    def y_dev(other):
        return ((other // NYLO) * NCORE + core, z, (other % NYLO) * NX + x)

    def final_dev(other, other_core):
        return ((other // NYLO) * NCORE + other_core, z, (other % NYLO) * NX + x)

    def x_dev(other):
        return (dp, z, ylo * NX + other)

    def z_dev(other):
        return (dp, other, hid)

    next_dev = (z_dev((z + 1) % NZ), z_dev((z + NZ - 1) % NZ))
    sent = []

    def send(src, dst, s, r, dev):
        copy = pltpu.make_async_remote_copy(
            src_ref=src, dst_ref=dst, send_sem=s, recv_sem=r,
            device_id=dev, device_id_type=pl.DeviceIdType.MESH,
        )
        copy.start()
        sent.append(copy)

    def arrived(dst, s, r):
        pltpu.make_async_remote_copy(
            src_ref=dst, dst_ref=dst, send_sem=s, recv_sem=r,
            device_id=sibling, device_id_type=pl.DeviceIdType.MESH,
        ).wait_recv()

    own_cot = xc.at[yhi, core, ylo, x, 1]
    loads = {}
    for i, (src, dst) in enumerate((
        (tok_hbm, tok_ref), (cot_hbm, own_cot), (job_hbm, job_ref), (a_hbm, a_ref),
        (gut_hbm, gut_ref), (dn_hbm, dn_ref), (bt_hbm, bt_ref),
    )):
        loads[i] = pltpu.make_async_copy(src, dst, load_s.at[i])
        loads[i].start()
    stores = []

    def store(i, src, dst):
        copy = pltpu.make_async_copy(src, dst, store_s.at[i])
        copy.start()
        stores.append(copy)

    barrier = pltpu.get_barrier_semaphore()
    partners = [sibling]
    partners += [y_dev((y + k) % NY) for k in range(1, NY)]
    partners += [final_dev((y + k) % NY, 1 - core) for k in range(1, NY)]
    partners += [x_dev((x + k) % NX) for k in range(1, NX)]
    partners += [z_dev((z + k) % NZ) for k in range(1, NZ)]
    for dev in partners:
        pl.semaphore_signal(barrier, inc=1, device_id=dev, device_id_type=pl.DeviceIdType.MESH)
    eye = (
        lax.broadcasted_iota(jnp.int32, (256, 256), 0)
        == lax.broadcasted_iota(jnp.int32, (256, 256), 1)
    ).astype(F32).astype(BF16)

    def turned(ref):
        cols = ref.shape[1]
        return jnp.concatenate(
            [mm_nt(eye, ref[:, i:i + 256]) for i in range(0, cols, 256)], axis=0
        ).astype(BF16)

    loads[0].wait()
    xc[yhi, core, :, :, 0] = turned(tok_ref).reshape(NYLO, NX, PIECE, JOB_ROWS)
    loads[1].wait()
    loads[2].wait()
    jobs[yhi, core] = jnp.broadcast_to(job_ref[...].astype(F32), (16, JOB_ROWS)).astype(BF16)
    pl.semaphore_wait(barrier, len(partners))

    def piece(k, src, low, at_x):
        view = xc.at[src, core, low, at_x]
        return view if k else xc.at[src, core, low, at_x, 1]

    both_low = pl.ds(0, NYLO)
    order = (0, 1, 3, 2)
    source = [(yhi + NYHI - k) % NYHI for k in range(NYHI)]
    own = xc.at[yhi, core, ylo, x]
    send(own_cot, own_cot, ty_s.at[0, 0], ty_r.at[0, 0], y_dev(yhi * NYLO + 1 - ylo))
    for k in order[1:]:
        for low in range(NYLO):
            dev = y_dev(((yhi + k) % NYHI) * NYLO + low)
            send(own, own, ty_s.at[k, low], ty_r.at[k, ylo], dev)
    own = xc.at[yhi, core, :, :, 0]
    send(own, own, tc_s.at[NYHI], tc_r.at[NYHI], sibling)
    own = jobs.at[yhi, core]
    for k in range(1, NYHI):
        dev = y_dev(((yhi + k) % NYHI) * NYLO + ylo)
        send(own, own, jy_s.at[k - 1], jy_r.at[k - 1], dev)
    loads[3].wait()
    for k in range(2):
        at[k * JOB_COLS:(k + 1) * JOB_COLS, :] = turned(a_ref.at[k])
    x_next = (x_dev((x + 1) % NX), x_dev((x + NX - 1) % NX))
    x_from = ((x + NX - 1) % NX, (x + 1) % NX)
    for k in order:
        src = source[k]
        if k == 0:
            arrived(piece(0, src, 1 - ylo, x), ty_s.at[0, 0], ty_r.at[0, 0])
        else:
            for low in range(NYLO):
                arrived(piece(k, src, low, x), ty_s.at[k, low], ty_r.at[k, low])
        for way in range(2):
            own = piece(k, src, both_low, x)
            send(own, own, tx_s.at[k, way], tx_r.at[k, way], x_next[way])
    for k in range(1, NYHI):
        arrived(jobs.at[source[k], core], jy_s.at[k - 1], jy_r.at[k - 1])
    send(jobs.at[:, core], jobs.at[:, core], jc_s.at[0], jc_r.at[0], sibling)
    for i in range(4, 7):
        loads[i].wait()
    for k in range(2):
        gu[k] = turned(gut_ref.at[k])
        bn[k] = turned(bt_ref.at[k])
    dnt[...] = turned(dn_ref)
    for k in order:
        for way in range(2):
            arrived(piece(k, source[k], both_low, x_from[way]), tx_s.at[k, way], tx_r.at[k, way])
            onward = piece(k, source[k], way, x_from[way])
            send(onward, onward, tf_s.at[k, way], tf_r.at[k, way], x_next[way])
    for k in order:
        for way in range(2):
            across = piece(k, source[k], way, (x + 2) % NX)
            arrived(across, tf_s.at[k, way], tf_r.at[k, way])
        whole = xc.at[source[k], core] if k else xc.at[yhi, core, :, :, 1]
        send(whole, whole, tc_s.at[k], tc_r.at[k], sibling)
    arrived(jobs.at[:, 1 - core], jc_s.at[0], jc_r.at[0])
    arrived(xc.at[yhi, 1 - core, :, :, 0], tc_s.at[NYHI], tc_r.at[NYHI])
    for k in order:
        whole = xc.at[source[k], 1 - core] if k else xc.at[yhi, 1 - core, :, :, 1]
        arrived(whole, tc_s.at[k], tc_r.at[k])

    def wide_mask(row):
        row = row.astype(F32)[0:1]
        col = lax.broadcasted_iota(jnp.int32, (JOB_COLS, row.shape[1]), 0) // ADAPTER_RANK
        return col.astype(F32) == row

    def pair(kind, q):
        return jnp.concatenate(
            [xc[q, c, :, :, kind].reshape(FEAT, JOB_ROWS) for c in range(NCORE)], axis=1
        )

    def pair_mask(q):
        return wide_mask(jnp.concatenate([jobs[q, c] for c in range(NCORE)], axis=1))

    def forward_sums(q):
        rows = pair(0, q)
        mask = pair_mask(q)
        pre = [mm(gut_ref[k], rows) for k in range(2)]
        low = mm(at[...], rows)
        for k in range(2):
            picked = jnp.where(mask, low[k * JOB_COLS:(k + 1) * JOB_COLS], 0.0)
            picked = picked.reshape(JOB_COUNT, ADAPTER_RANK, 2 * JOB_ROWS).sum(0)
            low_at = LOW_AT + k * ADAPTER_RANK
            for c in range(NCORE):
                cut = slice(c * JOB_ROWS, (c + 1) * JOB_ROWS)
                part[NCORE * q + c, k * HID:(k + 1) * HID, :] = pre[k][:, cut]
                part[NCORE * q + c, low_at:low_at + ADAPTER_RANK, :] = picked[:, cut]

    def backward_sums(q):
        back = mm(dn_ref[...], pair(1, q))
        for c in range(NCORE):
            part[NCORE * q + c, BACK_AT:, :] = back[:, c * JOB_ROWS:(c + 1) * JOB_ROWS]

    def sum_step(t, chunks):
        ready = []
        for way in range(2):
            cuts = [c for c in chunks if t > 0 or c % 2 == way]
            cuts.sort(key=lambda c: (c // 2 if t > 1 else 0, c % 2 == way))
            ready.append(cuts)
        for cuts in zip(*ready):
            for way, c in enumerate(cuts):
                block = (z + 4 - t) % NZ if way == 0 else (z + 4 + t) % NZ
                lo, hi = SUMS[c]
                value = part[block, lo:hi, :]
                if t > 1 or (t == 1 and c % 2 == way):
                    before = ring_in.at[way, t - 1, lo:hi]
                    arrived(before, rs_s.at[way, t - 1, c], rs_r.at[way, t - 1, c])
                    value = value + before[...].astype(F32)
                ring_out[way, t, lo:hi, :] = value.astype(BF16)
                send(ring_out.at[way, t, lo:hi], ring_in.at[way, t, lo:hi],
                     rs_s.at[way, t, c], rs_r.at[way, t, c], next_dev[way])

    def sum_end(chunks):
        for c in chunks:
            lo, hi = SUMS[c]
            for way in range(2):
                arrived(ring_in.at[way, 3, lo:hi], rs_s.at[way, 3, c], rs_r.at[way, 3, c])
        lo, hi = SUMS[chunks[0]][0], SUMS[chunks[-1]][1]
        return part[z, lo:hi, :] + (
            ring_in[0, 3, lo:hi, :].astype(F32) + ring_in[1, 3, lo:hi, :].astype(F32)
        )

    def gather_step(t, chunks):
        for c in chunks:
            lo, hi = PARTS[c]
            for way in range(2):
                block = (z + NZ - t) % NZ if way == 0 else (z + t) % NZ
                piece = held.at[block, lo:hi]
                if t > 0:
                    arrived(piece, zg_s.at[way, t - 1, c], zg_r.at[way, t - 1, c])
                if t < 3 or c % 2 == way:
                    send(piece, piece, zg_s.at[way, t, c], zg_r.at[way, t, c], next_dev[way])

    def gather_end(chunks):
        for c in chunks:
            lo, hi = PARTS[c]
            arrived(held.at[far, lo:hi], zg_s.at[c % 2, 3, c], zg_r.at[c % 2, 3, c])

    def blocks_at(t):
        if t == 0 or t == 4:
            return [(z + t) % NZ]
        return [(z + NZ - t) % NZ, (z + t) % NZ]

    def held_rows(blocks, lo, hi):
        return jnp.concatenate([held[p, lo:hi, :] for p in blocks], axis=1)

    def slots(t):
        first = (0, 1, 3, 5, 7)[t]
        return [(first + i, p) for i, p in enumerate(blocks_at(t))]

    def core_stage(t):
        blocks = blocks_at(t)
        values = (
            mm(dnt[...], held_rows(blocks, 0, HID)),
            mm(gu[0], held_rows(blocks, GRAD_AT, GRAD_AT + HID))
            + mm(gu[1], held_rows(blocks, GRAD_AT + HID, ROWS)),
        )
        for j, (n, _) in enumerate(slots(t)):
            for i in range(2):
                cut = values[i][:, j * JOB_ROWS:(j + 1) * JOB_ROWS].astype(BF16)
                outp[n, i] = cut.reshape(NYLO, NX, PIECE, JOB_ROWS)
            send(outp.at[n, 1 - core], core_in.at[n], oc_s.at[n], oc_r.at[n], sibling)

    def x_stage(t):
        for n, _ in slots(t):
            arrived(core_in.at[n], oc_s.at[n], oc_r.at[n])
            x_out[n] = (outp[n, core].astype(F32) + core_in[n].astype(F32)).astype(BF16)
            for k in range(1, NX):
                other = (x + k) % NX
                send(x_out.at[n, :, other], x_in.at[n, k - 1],
                     ox_s.at[n, k - 1], ox_r.at[n, k - 1], x_dev(other))

    def y_copies(n, p):
        for low in range(NYLO):
            other = (p // NCORE) * NYLO + low
            k = (other + NY - y) % NY
            here = (p == dp) & (low == ylo)
            yield low, here, pltpu.make_async_remote_copy(
                src_ref=y_out.at[n, low], dst_ref=y_in.at[core, k],
                send_sem=oy_s.at[n, low], recv_sem=oy_r.at[core, k],
                device_id=final_dev(other, p % NCORE), device_id_type=pl.DeviceIdType.MESH,
            )

    def y_stage(t):
        for n, p in slots(t):
            both = x_out[n, :, x].astype(F32)
            for k in range(1, NX):
                arrived(x_in.at[n, k - 1], ox_s.at[n, k - 1], ox_r.at[n, k - 1])
                both = both + x_in[n, k - 1].astype(F32)
            y_out[n] = both.astype(BF16)
            for low, here, copy in y_copies(n, p):
                @pl.when(jnp.logical_not(here))
                def _(copy=copy):
                    copy.start()

                @pl.when(here)
                def _(n=n, low=low):
                    fin[...] = y_out[n, low].astype(F32)

    forward, backward = (0, 1), (2, 3)
    every = forward + backward
    forward_sums(far // NCORE)
    backward_sums(far // NCORE)
    sum_step(0, every)

    @pl.loop(1, NYHI)
    def _(q):
        forward_sums((far // NCORE + q) % NYHI)
        backward_sums((far // NCORE + q) % NYHI)

    for t in range(1, 4):
        sum_step(t, every)

    total = sum_end(forward)
    mask = wide_mask(jobs[z // NCORE, z % NCORE])
    pre_act = []
    for k in range(2):
        low = total[LOW_AT + k * ADAPTER_RANK:LOW_AT + (k + 1) * ADAPTER_RANK]
        wide = jnp.where(mask, jnp.concatenate([low] * JOB_COUNT, axis=0), 0.0).astype(BF16)
        pre_act.append(total[k * HID:(k + 1) * HID] + SCALE * mm(bt_ref[k], wide))
    gate, up = pre_act
    sig = jax.nn.sigmoid(gate)
    silu = gate * sig
    held[z, 0:HID, :] = (silu * up).astype(BF16)
    held[z, HLOW_AT:GRAD_AT, :] = total[LOW_AT:BACK_AT].astype(BF16)
    gather_step(0, forward)
    back = sum_end(backward)
    grads = [
        (back * up * sig * (1.0 + gate * (1.0 - sig))).astype(BF16),
        (back * silu).astype(BF16),
    ]
    for k in range(2):
        held[z, GRAD_AT + k * HID:GRAD_AT + (k + 1) * HID, :] = grads[k]
    gather_step(0, backward)
    for k in range(2):
        wide = jnp.where(mask, mm(bn[k], grads[k]), 0.0)
        b_core_out[k * ADAPTER_RANK:(k + 1) * ADAPTER_RANK, :] = SCALE * wide.reshape(
            JOB_COUNT, ADAPTER_RANK, JOB_ROWS
        ).sum(0)
    send(b_core_out, b_core_in, bc_s.at[0], bc_r.at[0], sibling)
    core_stage(0)
    gather_step(1, every)
    core_stage(1)
    arrived(b_core_in, bc_s.at[0], bc_r.at[0])
    b_x_out[...] = b_core_out[...] + b_core_in[...]
    for k in range(1, NX):
        send(b_x_out, b_x_in.at[k - 1], bx_s.at[k - 1], bx_r.at[k - 1], x_dev((x + k) % NX))
    x_stage(0)
    gather_step(2, every)
    core_stage(2)
    both = b_x_out[...]
    for k in range(1, NX):
        arrived(b_x_in.at[k - 1], bx_s.at[k - 1], bx_r.at[k - 1])
        both = both + b_x_in[k - 1]
    b_y_out[...] = both
    for k in range(1, NY):
        send(b_y_out, b_y_in.at[k - 1], by_s.at[k - 1], by_r.at[k - 1], y_dev((y + k) % NY))
    x_stage(1)
    y_stage(0)
    gather_step(3, every)
    core_stage(3)
    both = b_y_out[...]
    for k in range(1, NY):
        arrived(b_y_in.at[k - 1], by_s.at[k - 1], by_r.at[k - 1])
        both = both + b_y_in[k - 1]
    inner[z] = both
    for k in range(1, NZ):
        send(inner.at[z], inner.at[z], bz_s.at[k - 1], bz_r.at[k - 1], z_dev((z + k) % NZ))
    x_stage(2)
    y_stage(1)
    gather_end(every)
    core_stage(4)
    x_stage(3)
    y_stage(2)

    x_stage(4)
    for k in range(2):
        acc = jnp.zeros((HID, JOB_COLS), F32)
        for q in range(NYHI):
            blocks = [NCORE * q + c for c in range(NCORE)]
            low_at, grad_at = HLOW_AT + k * ADAPTER_RANK, GRAD_AT + k * HID
            low = held_rows(blocks, low_at, low_at + ADAPTER_RANK).astype(F32)
            wide = jnp.where(pair_mask(q), jnp.concatenate([low] * JOB_COUNT, axis=0), 0.0)
            acc = acc + mm_nt(held_rows(blocks, grad_at, grad_at + HID), wide.astype(BF16))
        gb_ref[k] = SCALE * acc
    store(3, gb_ref, gb_hbm)
    y_stage(3)
    for k in range(1, NZ):
        arrived(inner.at[(z + NZ - k) % NZ], bz_s.at[k - 1], bz_r.at[k - 1])

    def wide_inner(k, blocks, mask):
        rows = [inner[p, k * ADAPTER_RANK:(k + 1) * ADAPTER_RANK, :] for p in blocks]
        rows = jnp.concatenate(rows, axis=1)
        wide = jnp.where(mask, jnp.concatenate([rows] * JOB_COUNT, axis=0), 0.0)
        hi = wide.astype(BF16)
        return hi, (wide - hi.astype(F32)).astype(BF16)

    for k in range(2):
        acc = jnp.zeros((FEAT, JOB_COLS), F32)
        for q in range(NYHI):
            rows = pair(0, q)
            for wide in wide_inner(k, [NCORE * q + c for c in range(NCORE)], pair_mask(q)):
                acc = acc + mm_nt(rows, wide)
        ga_ref[k] = acc
    store(2, ga_ref, ga_hbm)
    y_stage(4)
    mask = wide_mask(jobs[yhi, core])
    extra = jnp.zeros((PIECE, JOB_ROWS), F32)
    for k in range(2):
        cols = a_ref[k, pl.ds(pl.multiple_of(hid * PIECE, PIECE), PIECE), :]
        for wide in wide_inner(k, [dp], mask):
            extra = extra + mm(cols, wide)
    sums = []
    for c in range(NCORE):
        both = jnp.zeros((PIECE, JOB_ROWS), F32)
        for k in range(1, NY):
            arrived(y_in.at[c, k], oy_s.at[0, 0], oy_r.at[c, k])
            both = both + y_in[c, k].astype(F32)
        sums.append(both)
    arrived(y_in.at[1 - core, 0], oy_s.at[0, 0], oy_r.at[1 - core, 0])
    near = y_in[1 - core, 0].astype(F32)
    mixed_ref[...] = (sums[0] + jnp.where(core == 0, fin[...], near)).astype(BF16)
    ig_ref[...] = (sums[1] + extra + jnp.where(core == 0, near, fin[...])).astype(BF16)
    store(0, mixed_ref, mixed_hbm)
    store(1, ig_ref, ig_hbm)
    for t in range(5):
        for n, p in slots(t):
            for _, here, copy in y_copies(n, p):
                @pl.when(jnp.logical_not(here))
                def _(copy=copy):
                    copy.wait_send()
    for copy in stores:
        copy.wait()
    for copy in sent:
        copy.wait_send()


def hand_over(*refs):
    srcs, dsts, held = refs[0:4], refs[4:8], refs[8:12]
    load_sem, store_sem = refs[12:14]
    loads = [pltpu.make_async_copy(srcs[i], held[i], load_sem.at[i]) for i in range(4)]
    stores = [pltpu.make_async_copy(held[i], dsts[i], store_sem.at[i]) for i in range(4)]
    for copy in loads:
        copy.start()
    for load, copy in zip(loads, stores):
        load.wait()
        copy.start()
    for copy in stores:
        copy.wait()


def local(tokens, token_job_index, gate_up, down, adapter_in, adapter_out, cotangent):
    hbm = pl.BlockSpec(memory_space=pltpu.HBM)
    buf = pltpu.VMEM
    tile = (PIECE, JOB_ROWS)
    ring = (2, 4, 4)
    sems = [
        (NYHI, NYLO), (NYHI, 2), (NYHI, 2), (NYHI + 1,), (NYHI - 1,), (1,),
        ring, ring, (NZ,), (NZ, NX - 1), None,
        (1,), (NX - 1,), (NY - 1,), (NZ - 1,),
    ]
    sems = [(s, s) if s else ((NZ, NYLO), (NCORE, NY)) for s in sems]
    outs = pl.pallas_call(
        kernel,
        out_shape=[
            jax.ShapeDtypeStruct(tile, BF16),
            jax.ShapeDtypeStruct(tile, BF16),
            jax.ShapeDtypeStruct((2, FEAT, JOB_COLS), F32),
            jax.ShapeDtypeStruct((2, HID, JOB_COLS), F32),
        ],
        in_specs=[hbm] * 7,
        out_specs=[hbm] * 4,
        scratch_shapes=[
            buf((JOB_ROWS, FEAT), BF16),
            buf((1, JOB_ROWS), jnp.int32),
            buf((2, HID, FEAT), BF16),
            buf((HID, FEAT), BF16),
            buf((2, FEAT, JOB_COLS), BF16),
            buf((2, HID, JOB_COLS), BF16),
            buf(tile, BF16),
            buf(tile, BF16),
            buf((2, FEAT, JOB_COLS), F32),
            buf((2, HID, JOB_COLS), F32),
            buf((NYHI, NCORE, NYLO, NX, 2) + tile, BF16),
            buf((NYHI, NCORE, 16, JOB_ROWS), BF16),
            buf((2, FEAT, HID), BF16),
            buf((FEAT, HID), BF16),
            buf((2 * JOB_COLS, FEAT), BF16),
            buf((2, JOB_COLS, HID), BF16),
            buf((NZ, ROWS, JOB_ROWS), F32),
            buf((2, 4, ROWS, JOB_ROWS), BF16),
            buf((2, 4, ROWS, JOB_ROWS), BF16),
            buf((NZ, ROWS, JOB_ROWS), BF16),
            buf((NZ, 2, NYLO, NX) + tile, BF16),
            buf((NZ, NYLO, NX) + tile, BF16),
            buf((NZ, NYLO, NX) + tile, BF16),
            buf((NZ, NX - 1, NYLO) + tile, BF16),
            buf((NZ, NYLO) + tile, BF16),
            buf((NCORE, NY) + tile, BF16),
            buf(tile, F32),
            buf((LOW, JOB_ROWS), F32),
            buf((LOW, JOB_ROWS), F32),
            buf((LOW, JOB_ROWS), F32),
            buf((NX - 1, LOW, JOB_ROWS), F32),
            buf((LOW, JOB_ROWS), F32),
            buf((NY - 1, LOW, JOB_ROWS), F32),
            buf((NZ, LOW, JOB_ROWS), F32),
        ] + [pltpu.SemaphoreType.DMA(s) for pair in sems for s in pair] + [
            pltpu.SemaphoreType.DMA((7,)), pltpu.SemaphoreType.DMA((4,)),
        ],
        compiler_params=pltpu.CompilerParams(
            collective_id=0, has_side_effects=True, vmem_limit_bytes=63 * 1024 * 1024
        ),
    )(
        tokens, token_job_index.reshape(1, JOB_ROWS), jnp.swapaxes(gate_up, 1, 2), down,
        adapter_in, jnp.swapaxes(adapter_out, 1, 2), cotangent.T,
    )
    dma = pltpu.SemaphoreType.DMA((4,))
    mixed, grad, grad_in, grad_out = pl.pallas_call(
        hand_over,
        out_shape=[jax.ShapeDtypeStruct(out.shape, out.dtype) for out in outs],
        in_specs=[hbm] * 4,
        out_specs=[hbm] * 4,
        scratch_shapes=[buf(out.shape, out.dtype) for out in outs] + [dma, dma],
        compiler_params=pltpu.CompilerParams(vmem_limit_bytes=63 * 1024 * 1024),
    )(*outs)
    return mixed.T, grad.T, grad_in, jnp.swapaxes(grad_out, 1, 2)


def solution(mesh):
    return jax.shard_map(
        local,
        mesh=mesh,
        in_specs=(
            P("dp", "width"),
            P("dp"),
            P(None, "width", ("dp", "hidden")),
            P(("dp", "hidden"), "width"),
            P(None, "width", None),
            P(None, None, ("dp", "hidden")),
            P("dp", ("width", "hidden")),
        ),
        out_specs=(
            P("dp", ("width", "hidden")),
            P("dp", ("width", "hidden")),
            P(None, "width", None),
            P(None, None, ("dp", "hidden")),
        ),
        check_vma=False,
    )
```

```python
import jax
import jax.numpy as jnp
from jax import lax
from jax.experimental import pallas as pl
from jax.experimental.pallas import tpu as pltpu
from jax.sharding import PartitionSpec as P

JOB_COUNT = 16
ADAPTER_RANK = 16
JOB_COLS = JOB_COUNT * ADAPTER_RANK
JOB_ROWS = 128
SCALE = 0.5
F32 = jnp.float32
BF16 = jnp.bfloat16

NX, NYLO, NYHI, NCORE, NZ = 4, 2, 4, 2, 8
NY = NYLO * NYHI
PIECE = 64
FEAT = NX * NYLO * PIECE
HID = 224
LOW = 2 * ADAPTER_RANK
SUMS = ((0, 240), (240, 480), (480, 592), (592, 704))
LOW_AT, BACK_AT = 2 * HID, 2 * HID + LOW
PARTS = ((0, 128), (128, 256), (256, 480), (480, 704))
HLOW_AT, GRAD_AT = HID, HID + LOW
ROWS = 3 * HID + LOW


def mm(a, b):
    return jnp.dot(a, b, preferred_element_type=F32)


def mm_nt(a, b):
    return lax.dot_general(a, b, (((1,), (1,)), ((), ())), preferred_element_type=F32)


def kernel(
    tok_hbm, job_hbm, gut_hbm, dn_hbm, a_hbm, bt_hbm, cot_hbm,
    mixed_hbm, ig_hbm, ga_hbm, gb_hbm,
    tok_ref, job_ref, gut_ref, dn_ref, a_ref, bt_ref,
    mixed_ref, ig_ref, ga_ref, gb_ref,
    xc, jobs, gu, dnt, at, bn,
    part, ring_out, ring_in, held,
    outp, core_in, x_out, x_in, y_out, y_in, fin,
    b_core_out, b_core_in, b_x_out, b_x_in, b_y_out, b_y_in, inner,
    ty_s, ty_r, tx_s, tx_r, tf_s, tf_r, tc_s, tc_r, jy_s, jy_r, jc_s, jc_r,
    rs_s, rs_r, zg_s, zg_r, oc_s, oc_r, ox_s, ox_r, oy_s, oy_r,
    bc_s, bc_r, bx_s, bx_r, by_s, by_r, bz_s, bz_r, load_s, store_s,
):
    dp = lax.axis_index("dp")
    z = lax.axis_index("width")
    hid = lax.axis_index("hidden")
    yhi, core = dp // NCORE, dp % NCORE
    ylo, x = hid // NX, hid % NX
    y = yhi * NYLO + ylo
    sibling = (yhi * NCORE + 1 - core, z, hid)
    far = (z + NZ // 2) % NZ

    def y_dev(other):
        return ((other // NYLO) * NCORE + core, z, (other % NYLO) * NX + x)

    def final_dev(other, other_core):
        return ((other // NYLO) * NCORE + other_core, z, (other % NYLO) * NX + x)

    def x_dev(other):
        return (dp, z, ylo * NX + other)

    def z_dev(other):
        return (dp, other, hid)

    next_dev = (z_dev((z + 1) % NZ), z_dev((z + NZ - 1) % NZ))
    sent = []

    def send(src, dst, s, r, dev):
        copy = pltpu.make_async_remote_copy(
            src_ref=src, dst_ref=dst, send_sem=s, recv_sem=r,
            device_id=dev, device_id_type=pl.DeviceIdType.MESH,
        )
        copy.start()
        sent.append(copy)

    def arrived(dst, s, r):
        pltpu.make_async_remote_copy(
            src_ref=dst, dst_ref=dst, send_sem=s, recv_sem=r,
            device_id=sibling, device_id_type=pl.DeviceIdType.MESH,
        ).wait_recv()

    own_cot = xc.at[yhi, core, ylo, x, 1]
    loads = {}
    for i, (src, dst) in enumerate((
        (tok_hbm, tok_ref), (cot_hbm, own_cot), (job_hbm, job_ref), (a_hbm, a_ref),
        (gut_hbm, gut_ref), (dn_hbm, dn_ref), (bt_hbm, bt_ref),
    )):
        loads[i] = pltpu.make_async_copy(src, dst, load_s.at[i])
        loads[i].start()
    stores = []

    def store(i, src, dst):
        copy = pltpu.make_async_copy(src, dst, store_s.at[i])
        copy.start()
        stores.append(copy)

    barrier = pltpu.get_barrier_semaphore()
    partners = [sibling]
    partners += [y_dev((y + k) % NY) for k in range(1, NY)]
    partners += [final_dev((y + k) % NY, 1 - core) for k in range(1, NY)]
    partners += [x_dev((x + k) % NX) for k in range(1, NX)]
    partners += [z_dev((z + k) % NZ) for k in range(1, NZ)]
    for dev in partners:
        pl.semaphore_signal(barrier, inc=1, device_id=dev, device_id_type=pl.DeviceIdType.MESH)
    eye = (
        lax.broadcasted_iota(jnp.int32, (256, 256), 0)
        == lax.broadcasted_iota(jnp.int32, (256, 256), 1)
    ).astype(F32).astype(BF16)

    def turned(ref):
        cols = ref.shape[1]
        return jnp.concatenate(
            [mm_nt(eye, ref[:, i:i + 256]) for i in range(0, cols, 256)], axis=0
        ).astype(BF16)

    loads[0].wait()
    xc[yhi, core, :, :, 0] = turned(tok_ref).reshape(NYLO, NX, PIECE, JOB_ROWS)
    loads[1].wait()
    loads[2].wait()
    jobs[yhi, core] = jnp.broadcast_to(job_ref[...].astype(F32), (16, JOB_ROWS)).astype(BF16)
    pl.semaphore_wait(barrier, len(partners))

    def piece(k, src, low, at_x):
        view = xc.at[src, core, low, at_x]
        return view if k else xc.at[src, core, low, at_x, 1]

    both_low = pl.ds(0, NYLO)
    order = (0, 1, 3, 2)
    source = [(yhi + NYHI - k) % NYHI for k in range(NYHI)]
    own = xc.at[yhi, core, ylo, x]
    send(own_cot, own_cot, ty_s.at[0, 0], ty_r.at[0, 0], y_dev(yhi * NYLO + 1 - ylo))
    for k in order[1:]:
        for low in range(NYLO):
            dev = y_dev(((yhi + k) % NYHI) * NYLO + low)
            send(own, own, ty_s.at[k, low], ty_r.at[k, ylo], dev)
    own = xc.at[yhi, core, :, :, 0]
    send(own, own, tc_s.at[NYHI], tc_r.at[NYHI], sibling)
    own = jobs.at[yhi, core]
    for k in range(1, NYHI):
        dev = y_dev(((yhi + k) % NYHI) * NYLO + ylo)
        send(own, own, jy_s.at[k - 1], jy_r.at[k - 1], dev)
    loads[3].wait()
    for k in range(2):
        at[k * JOB_COLS:(k + 1) * JOB_COLS, :] = turned(a_ref.at[k])
    x_next = (x_dev((x + 1) % NX), x_dev((x + NX - 1) % NX))
    x_from = ((x + NX - 1) % NX, (x + 1) % NX)
    for k in order:
        src = source[k]
        if k == 0:
            arrived(piece(0, src, 1 - ylo, x), ty_s.at[0, 0], ty_r.at[0, 0])
        else:
            for low in range(NYLO):
                arrived(piece(k, src, low, x), ty_s.at[k, low], ty_r.at[k, low])
        for way in range(2):
            own = piece(k, src, both_low, x)
            send(own, own, tx_s.at[k, way], tx_r.at[k, way], x_next[way])
    for k in range(1, NYHI):
        arrived(jobs.at[source[k], core], jy_s.at[k - 1], jy_r.at[k - 1])
    send(jobs.at[:, core], jobs.at[:, core], jc_s.at[0], jc_r.at[0], sibling)
    for i in range(4, 7):
        loads[i].wait()
    for k in range(2):
        gu[k] = turned(gut_ref.at[k])
        bn[k] = turned(bt_ref.at[k])
    dnt[...] = turned(dn_ref)
    for k in order:
        for way in range(2):
            arrived(piece(k, source[k], both_low, x_from[way]), tx_s.at[k, way], tx_r.at[k, way])
            onward = piece(k, source[k], way, x_from[way])
            send(onward, onward, tf_s.at[k, way], tf_r.at[k, way], x_next[way])
    for k in order:
        for way in range(2):
            across = piece(k, source[k], way, (x + 2) % NX)
            arrived(across, tf_s.at[k, way], tf_r.at[k, way])
        whole = xc.at[source[k], core] if k else xc.at[yhi, core, :, :, 1]
        send(whole, whole, tc_s.at[k], tc_r.at[k], sibling)
    arrived(jobs.at[:, 1 - core], jc_s.at[0], jc_r.at[0])
    arrived(xc.at[yhi, 1 - core, :, :, 0], tc_s.at[NYHI], tc_r.at[NYHI])
    for k in order:
        whole = xc.at[source[k], 1 - core] if k else xc.at[yhi, 1 - core, :, :, 1]
        arrived(whole, tc_s.at[k], tc_r.at[k])

    def wide_mask(row):
        row = row.astype(F32)[0:1]
        col = lax.broadcasted_iota(jnp.int32, (JOB_COLS, row.shape[1]), 0) // ADAPTER_RANK
        return col.astype(F32) == row

    def pair(kind, q):
        return jnp.concatenate(
            [xc[q, c, :, :, kind].reshape(FEAT, JOB_ROWS) for c in range(NCORE)], axis=1
        )

    def pair_mask(q):
        return wide_mask(jnp.concatenate([jobs[q, c] for c in range(NCORE)], axis=1))

    def forward_sums(q):
        rows = pair(0, q)
        mask = pair_mask(q)
        pre = [mm(gut_ref[k], rows) for k in range(2)]
        low = mm(at[...], rows)
        for k in range(2):
            picked = jnp.where(mask, low[k * JOB_COLS:(k + 1) * JOB_COLS], 0.0)
            picked = picked.reshape(JOB_COUNT, ADAPTER_RANK, 2 * JOB_ROWS).sum(0)
            low_at = LOW_AT + k * ADAPTER_RANK
            for c in range(NCORE):
                cut = slice(c * JOB_ROWS, (c + 1) * JOB_ROWS)
                part[NCORE * q + c, k * HID:(k + 1) * HID, :] = pre[k][:, cut]
                part[NCORE * q + c, low_at:low_at + ADAPTER_RANK, :] = picked[:, cut]

    def backward_sums(q):
        back = mm(dn_ref[...], pair(1, q))
        for c in range(NCORE):
            part[NCORE * q + c, BACK_AT:, :] = back[:, c * JOB_ROWS:(c + 1) * JOB_ROWS]

    def sum_step(t, chunks):
        ready = []
        for way in range(2):
            cuts = [c for c in chunks if t > 0 or c % 2 == way]
            cuts.sort(key=lambda c: (c // 2 if t > 1 else 0, c % 2 == way))
            ready.append(cuts)
        for cuts in zip(*ready):
            for way, c in enumerate(cuts):
                block = (z + 4 - t) % NZ if way == 0 else (z + 4 + t) % NZ
                lo, hi = SUMS[c]
                value = part[block, lo:hi, :]
                if t > 1 or (t == 1 and c % 2 == way):
                    before = ring_in.at[way, t - 1, lo:hi]
                    arrived(before, rs_s.at[way, t - 1, c], rs_r.at[way, t - 1, c])
                    value = value + before[...].astype(F32)
                ring_out[way, t, lo:hi, :] = value.astype(BF16)
                send(ring_out.at[way, t, lo:hi], ring_in.at[way, t, lo:hi],
                     rs_s.at[way, t, c], rs_r.at[way, t, c], next_dev[way])

    def sum_end(chunks):
        for c in chunks:
            lo, hi = SUMS[c]
            for way in range(2):
                arrived(ring_in.at[way, 3, lo:hi], rs_s.at[way, 3, c], rs_r.at[way, 3, c])
        lo, hi = SUMS[chunks[0]][0], SUMS[chunks[-1]][1]
        return part[z, lo:hi, :] + (
            ring_in[0, 3, lo:hi, :].astype(F32) + ring_in[1, 3, lo:hi, :].astype(F32)
        )

    def gather_step(t, chunks):
        for c in chunks:
            lo, hi = PARTS[c]
            for way in range(2):
                block = (z + NZ - t) % NZ if way == 0 else (z + t) % NZ
                piece = held.at[block, lo:hi]
                if t > 0:
                    arrived(piece, zg_s.at[way, t - 1, c], zg_r.at[way, t - 1, c])
                if t < 3 or c % 2 == way:
                    send(piece, piece, zg_s.at[way, t, c], zg_r.at[way, t, c], next_dev[way])

    def gather_end(chunks):
        for c in chunks:
            lo, hi = PARTS[c]
            arrived(held.at[far, lo:hi], zg_s.at[c % 2, 3, c], zg_r.at[c % 2, 3, c])

    def blocks_at(t):
        if t == 0 or t == 4:
            return [(z + t) % NZ]
        return [(z + NZ - t) % NZ, (z + t) % NZ]

    def held_rows(blocks, lo, hi):
        return jnp.concatenate([held[p, lo:hi, :] for p in blocks], axis=1)

    def slots(t):
        first = (0, 1, 3, 5, 7)[t]
        return [(first + i, p) for i, p in enumerate(blocks_at(t))]

    def core_stage(t):
        blocks = blocks_at(t)
        values = (
            mm(dnt[...], held_rows(blocks, 0, HID)),
            mm(gu[0], held_rows(blocks, GRAD_AT, GRAD_AT + HID))
            + mm(gu[1], held_rows(blocks, GRAD_AT + HID, ROWS)),
        )
        for j, (n, _) in enumerate(slots(t)):
            for i in range(2):
                cut = values[i][:, j * JOB_ROWS:(j + 1) * JOB_ROWS].astype(BF16)
                outp[n, i] = cut.reshape(NYLO, NX, PIECE, JOB_ROWS)
            send(outp.at[n, 1 - core], core_in.at[n], oc_s.at[n], oc_r.at[n], sibling)

    def x_stage(t):
        for n, _ in slots(t):
            arrived(core_in.at[n], oc_s.at[n], oc_r.at[n])
            x_out[n] = (outp[n, core].astype(F32) + core_in[n].astype(F32)).astype(BF16)
            for k in range(1, NX):
                other = (x + k) % NX
                send(x_out.at[n, :, other], x_in.at[n, k - 1],
                     ox_s.at[n, k - 1], ox_r.at[n, k - 1], x_dev(other))

    def y_copies(n, p):
        for low in range(NYLO):
            other = (p // NCORE) * NYLO + low
            k = (other + NY - y) % NY
            here = (p == dp) & (low == ylo)
            yield low, here, pltpu.make_async_remote_copy(
                src_ref=y_out.at[n, low], dst_ref=y_in.at[core, k],
                send_sem=oy_s.at[n, low], recv_sem=oy_r.at[core, k],
                device_id=final_dev(other, p % NCORE), device_id_type=pl.DeviceIdType.MESH,
            )

    def y_stage(t):
        for n, p in slots(t):
            both = x_out[n, :, x].astype(F32)
            for k in range(1, NX):
                arrived(x_in.at[n, k - 1], ox_s.at[n, k - 1], ox_r.at[n, k - 1])
                both = both + x_in[n, k - 1].astype(F32)
            y_out[n] = both.astype(BF16)
            for low, here, copy in y_copies(n, p):
                @pl.when(jnp.logical_not(here))
                def _(copy=copy):
                    copy.start()

                @pl.when(here)
                def _(n=n, low=low):
                    fin[...] = y_out[n, low].astype(F32)

    forward, backward = (0, 1), (2, 3)
    every = forward + backward
    forward_sums(far // NCORE)
    backward_sums(far // NCORE)
    sum_step(0, every)

    @pl.loop(1, NYHI)
    def _(q):
        forward_sums((far // NCORE + q) % NYHI)
        backward_sums((far // NCORE + q) % NYHI)

    for t in range(1, 4):
        sum_step(t, every)

    total = sum_end(forward)
    mask = wide_mask(jobs[z // NCORE, z % NCORE])
    pre_act = []
    for k in range(2):
        low = total[LOW_AT + k * ADAPTER_RANK:LOW_AT + (k + 1) * ADAPTER_RANK]
        wide = jnp.where(mask, jnp.concatenate([low] * JOB_COUNT, axis=0), 0.0).astype(BF16)
        pre_act.append(total[k * HID:(k + 1) * HID] + SCALE * mm(bt_ref[k], wide))
    gate, up = pre_act
    sig = jax.nn.sigmoid(gate)
    silu = gate * sig
    held[z, 0:HID, :] = (silu * up).astype(BF16)
    held[z, HLOW_AT:GRAD_AT, :] = total[LOW_AT:BACK_AT].astype(BF16)
    gather_step(0, forward)
    back = sum_end(backward)
    grads = [
        (back * up * sig * (1.0 + gate * (1.0 - sig))).astype(BF16),
        (back * silu).astype(BF16),
    ]
    for k in range(2):
        held[z, GRAD_AT + k * HID:GRAD_AT + (k + 1) * HID, :] = grads[k]
    gather_step(0, backward)
    for k in range(2):
        wide = jnp.where(mask, mm(bn[k], grads[k]), 0.0)
        b_core_out[k * ADAPTER_RANK:(k + 1) * ADAPTER_RANK, :] = SCALE * wide.reshape(
            JOB_COUNT, ADAPTER_RANK, JOB_ROWS
        ).sum(0)
    send(b_core_out, b_core_in, bc_s.at[0], bc_r.at[0], sibling)
    core_stage(0)
    arrived(b_core_in, bc_s.at[0], bc_r.at[0])
    b_x_out[...] = b_core_out[...] + b_core_in[...]
    for k in range(1, NX):
        send(b_x_out, b_x_in.at[k - 1], bx_s.at[k - 1], bx_r.at[k - 1], x_dev((x + k) % NX))
    gather_step(1, every)
    core_stage(1)
    x_stage(0)
    both = b_x_out[...]
    for k in range(1, NX):
        arrived(b_x_in.at[k - 1], bx_s.at[k - 1], bx_r.at[k - 1])
        both = both + b_x_in[k - 1]
    b_y_out[...] = both
    for k in range(1, NY):
        send(b_y_out, b_y_in.at[k - 1], by_s.at[k - 1], by_r.at[k - 1], y_dev((y + k) % NY))
    gather_step(2, every)
    core_stage(2)
    x_stage(1)
    y_stage(0)
    gather_step(3, every)
    core_stage(3)
    x_stage(2)
    both = b_y_out[...]
    for k in range(1, NY):
        arrived(b_y_in.at[k - 1], by_s.at[k - 1], by_r.at[k - 1])
        both = both + b_y_in[k - 1]
    inner[z] = both
    for k in range(1, NZ):
        send(inner.at[z], inner.at[z], bz_s.at[k - 1], bz_r.at[k - 1], z_dev((z + k) % NZ))
    y_stage(1)
    gather_end(every)
    core_stage(4)
    x_stage(3)
    x_stage(4)
    y_stage(2)
    for k in range(2):
        acc = jnp.zeros((HID, JOB_COLS), F32)
        for q in range(NYHI):
            blocks = [NCORE * q + c for c in range(NCORE)]
            low_at, grad_at = HLOW_AT + k * ADAPTER_RANK, GRAD_AT + k * HID
            low = held_rows(blocks, low_at, low_at + ADAPTER_RANK).astype(F32)
            wide = jnp.where(pair_mask(q), jnp.concatenate([low] * JOB_COUNT, axis=0), 0.0)
            acc = acc + mm_nt(held_rows(blocks, grad_at, grad_at + HID), wide.astype(BF16))
        gb_ref[k] = SCALE * acc
    store(3, gb_ref, gb_hbm)
    y_stage(3)
    y_stage(4)
    for k in range(1, NZ):
        arrived(inner.at[(z + NZ - k) % NZ], bz_s.at[k - 1], bz_r.at[k - 1])

    def wide_inner(k, blocks, mask):
        rows = [inner[p, k * ADAPTER_RANK:(k + 1) * ADAPTER_RANK, :] for p in blocks]
        rows = jnp.concatenate(rows, axis=1)
        wide = jnp.where(mask, jnp.concatenate([rows] * JOB_COUNT, axis=0), 0.0)
        hi = wide.astype(BF16)
        return hi, (wide - hi.astype(F32)).astype(BF16)

    for k in range(2):
        acc = jnp.zeros((FEAT, JOB_COLS), F32)
        for q in range(NYHI):
            rows = pair(0, q)
            for wide in wide_inner(k, [NCORE * q + c for c in range(NCORE)], pair_mask(q)):
                acc = acc + mm_nt(rows, wide)
        ga_ref[k] = acc
    store(2, ga_ref, ga_hbm)
    mask = wide_mask(jobs[yhi, core])
    extra = jnp.zeros((PIECE, JOB_ROWS), F32)
    for k in range(2):
        cols = a_ref[k, pl.ds(pl.multiple_of(hid * PIECE, PIECE), PIECE), :]
        for wide in wide_inner(k, [dp], mask):
            extra = extra + mm(cols, wide)
    sums = []
    for c in range(NCORE):
        both = jnp.zeros((PIECE, JOB_ROWS), F32)
        for k in range(1, NY):
            arrived(y_in.at[c, k], oy_s.at[0, 0], oy_r.at[c, k])
            both = both + y_in[c, k].astype(F32)
        sums.append(both)
    arrived(y_in.at[1 - core, 0], oy_s.at[0, 0], oy_r.at[1 - core, 0])
    near = y_in[1 - core, 0].astype(F32)
    mixed_ref[...] = (sums[0] + jnp.where(core == 0, fin[...], near)).astype(BF16)
    ig_ref[...] = (sums[1] + extra + jnp.where(core == 0, near, fin[...])).astype(BF16)
    store(0, mixed_ref, mixed_hbm)
    store(1, ig_ref, ig_hbm)
    for t in range(5):
        for n, p in slots(t):
            for _, here, copy in y_copies(n, p):
                @pl.when(jnp.logical_not(here))
                def _(copy=copy):
                    copy.wait_send()
    for copy in stores:
        copy.wait()
    for copy in sent:
        copy.wait_send()


def hand_over(*refs):
    srcs, dsts, held = refs[0:4], refs[4:8], refs[8:12]
    load_sem, store_sem = refs[12:14]
    cuts = [(i, ()) for i in range(2)] + [
        (i, (k, pl.ds(j * rows, rows))) for i, rows in ((2, 256), (3, 112))
        for k in range(2) for j in range(2)
    ]
    loads, stores = [], []
    for n, (i, cut) in enumerate(cuts):
        src, own, dst = (ref.at[cut] if cut else ref for ref in (srcs[i], held[i], dsts[i]))
        loads.append(pltpu.make_async_copy(src, own, load_sem.at[n]))
        stores.append(pltpu.make_async_copy(own, dst, store_sem.at[n]))
        loads[-1].start()
    for load, copy in zip(loads, stores):
        load.wait()
        copy.start()
    for copy in stores:
        copy.wait()


def local(tokens, token_job_index, gate_up, down, adapter_in, adapter_out, cotangent):
    hbm = pl.BlockSpec(memory_space=pltpu.HBM)
    buf = pltpu.VMEM
    tile = (PIECE, JOB_ROWS)
    ring = (2, 4, 4)
    sems = [
        (NYHI, NYLO), (NYHI, 2), (NYHI, 2), (NYHI + 1,), (NYHI - 1,), (1,),
        ring, ring, (NZ,), (NZ, NX - 1), None,
        (1,), (NX - 1,), (NY - 1,), (NZ - 1,),
    ]
    sems = [(s, s) if s else ((NZ, NYLO), (NCORE, NY)) for s in sems]
    outs = pl.pallas_call(
        kernel,
        out_shape=[
            jax.ShapeDtypeStruct(tile, BF16),
            jax.ShapeDtypeStruct(tile, BF16),
            jax.ShapeDtypeStruct((2, FEAT, JOB_COLS), F32),
            jax.ShapeDtypeStruct((2, HID, JOB_COLS), F32),
        ],
        in_specs=[hbm] * 7,
        out_specs=[hbm] * 4,
        scratch_shapes=[
            buf((JOB_ROWS, FEAT), BF16),
            buf((1, JOB_ROWS), jnp.int32),
            buf((2, HID, FEAT), BF16),
            buf((HID, FEAT), BF16),
            buf((2, FEAT, JOB_COLS), BF16),
            buf((2, HID, JOB_COLS), BF16),
            buf(tile, BF16),
            buf(tile, BF16),
            buf((2, FEAT, JOB_COLS), F32),
            buf((2, HID, JOB_COLS), F32),
            buf((NYHI, NCORE, NYLO, NX, 2) + tile, BF16),
            buf((NYHI, NCORE, 16, JOB_ROWS), BF16),
            buf((2, FEAT, HID), BF16),
            buf((FEAT, HID), BF16),
            buf((2 * JOB_COLS, FEAT), BF16),
            buf((2, JOB_COLS, HID), BF16),
            buf((NZ, ROWS, JOB_ROWS), F32),
            buf((2, 4, ROWS, JOB_ROWS), BF16),
            buf((2, 4, ROWS, JOB_ROWS), BF16),
            buf((NZ, ROWS, JOB_ROWS), BF16),
            buf((NZ, 2, NYLO, NX) + tile, BF16),
            buf((NZ, NYLO, NX) + tile, BF16),
            buf((NZ, NYLO, NX) + tile, BF16),
            buf((NZ, NX - 1, NYLO) + tile, BF16),
            buf((NZ, NYLO) + tile, BF16),
            buf((NCORE, NY) + tile, BF16),
            buf(tile, F32),
            buf((LOW, JOB_ROWS), F32),
            buf((LOW, JOB_ROWS), F32),
            buf((LOW, JOB_ROWS), F32),
            buf((NX - 1, LOW, JOB_ROWS), F32),
            buf((LOW, JOB_ROWS), F32),
            buf((NY - 1, LOW, JOB_ROWS), F32),
            buf((NZ, LOW, JOB_ROWS), F32),
        ] + [pltpu.SemaphoreType.DMA(s) for pair in sems for s in pair] + [
            pltpu.SemaphoreType.DMA((7,)), pltpu.SemaphoreType.DMA((4,)),
        ],
        compiler_params=pltpu.CompilerParams(
            collective_id=0, has_side_effects=True, vmem_limit_bytes=63 * 1024 * 1024
        ),
    )(
        tokens, token_job_index.reshape(1, JOB_ROWS), jnp.swapaxes(gate_up, 1, 2), down,
        adapter_in, jnp.swapaxes(adapter_out, 1, 2), cotangent.T,
    )
    dma = pltpu.SemaphoreType.DMA((10,))
    mixed, grad, grad_in, grad_out = pl.pallas_call(
        hand_over,
        out_shape=[jax.ShapeDtypeStruct(out.shape, out.dtype) for out in outs],
        in_specs=[hbm] * 4,
        out_specs=[hbm] * 4,
        scratch_shapes=[buf(out.shape, out.dtype) for out in outs] + [dma, dma],
        compiler_params=pltpu.CompilerParams(vmem_limit_bytes=63 * 1024 * 1024),
    )(*outs)
    return mixed.T, grad.T, grad_in, jnp.swapaxes(grad_out, 1, 2)


def solution(mesh):
    return jax.shard_map(
        local,
        mesh=mesh,
        in_specs=(
            P("dp", "width"),
            P("dp"),
            P(None, "width", ("dp", "hidden")),
            P(("dp", "hidden"), "width"),
            P(None, "width", None),
            P(None, None, ("dp", "hidden")),
            P("dp", ("width", "hidden")),
        ),
        out_specs=(
            P("dp", ("width", "hidden")),
            P("dp", ("width", "hidden")),
            P(None, "width", None),
            P(None, None, ("dp", "hidden")),
        ),
        check_vma=False,
    )
```

```python
import jax
import jax.numpy as jnp
from jax import lax
from jax.experimental import pallas as pl
from jax.experimental.pallas import tpu as pltpu
from jax.sharding import PartitionSpec as P

JOB_COUNT = 16
ADAPTER_RANK = 16
JOB_COLS = JOB_COUNT * ADAPTER_RANK
JOB_ROWS = 128
SCALE = 0.5
F32 = jnp.float32
BF16 = jnp.bfloat16

NX, NYLO, NYHI, NCORE, NZ = 4, 2, 4, 2, 8
NY = NYLO * NYHI
PIECE = 64
FEAT = NX * NYLO * PIECE
HID = 224
LOW = 2 * ADAPTER_RANK
SUMS = ((0, 240), (240, 480), (480, 592), (592, 704))
LOW_AT, BACK_AT = 2 * HID, 2 * HID + LOW
PARTS = ((0, 128), (128, 256), (256, 480), (480, 704))
HLOW_AT, GRAD_AT = HID, HID + LOW
ROWS = 3 * HID + LOW


def mm(a, b):
    return jnp.dot(a, b, preferred_element_type=F32)


def mm_nt(a, b):
    return lax.dot_general(a, b, (((1,), (1,)), ((), ())), preferred_element_type=F32)


def kernel(
    tok_hbm, job_hbm, gut_hbm, dn_hbm, a_hbm, bt_hbm, cot_hbm,
    mixed_hbm, ig_hbm, ga_hbm, gb_hbm,
    tok_ref, job_ref, gut_ref, dn_ref, a_ref, bt_ref,
    mixed_ref, ig_ref, ga_ref, gb_ref,
    xc, jobs, gu, dnt, at, bn,
    part, ring_out, ring_in, held,
    outp, core_in, x_out, x_in, y_out, y_in, fin,
    b_core_out, b_core_in, b_x_out, b_x_in, b_y_out, b_y_in, inner,
    ty_s, ty_r, tx_s, tx_r, tf_s, tf_r, tc_s, tc_r, jy_s, jy_r, jc_s, jc_r,
    rs_s, rs_r, zg_s, zg_r, oc_s, oc_r, ox_s, ox_r, oy_s, oy_r,
    bc_s, bc_r, bx_s, bx_r, by_s, by_r, bz_s, bz_r, load_s, store_s,
):
    dp = lax.axis_index("dp")
    z = lax.axis_index("width")
    hid = lax.axis_index("hidden")
    yhi, core = dp // NCORE, dp % NCORE
    ylo, x = hid // NX, hid % NX
    y = yhi * NYLO + ylo
    sibling = (yhi * NCORE + 1 - core, z, hid)
    far = (z + NZ // 2) % NZ

    def y_dev(other):
        return ((other // NYLO) * NCORE + core, z, (other % NYLO) * NX + x)

    def final_dev(other, other_core):
        return ((other // NYLO) * NCORE + other_core, z, (other % NYLO) * NX + x)

    def x_dev(other):
        return (dp, z, ylo * NX + other)

    def z_dev(other):
        return (dp, other, hid)

    next_dev = (z_dev((z + 1) % NZ), z_dev((z + NZ - 1) % NZ))
    sent = []

    def send(src, dst, s, r, dev):
        copy = pltpu.make_async_remote_copy(
            src_ref=src, dst_ref=dst, send_sem=s, recv_sem=r,
            device_id=dev, device_id_type=pl.DeviceIdType.MESH,
        )
        copy.start()
        sent.append(copy)

    def arrived(dst, s, r):
        pltpu.make_async_remote_copy(
            src_ref=dst, dst_ref=dst, send_sem=s, recv_sem=r,
            device_id=sibling, device_id_type=pl.DeviceIdType.MESH,
        ).wait_recv()

    barrier = pltpu.get_barrier_semaphore()
    far_first = (4, 3, 5, 2, 6, 1, 7)
    partners = [z_dev((z + k) % NZ) for k in far_first]
    for k in far_first:
        partners += [y_dev((y + k) % NY), final_dev((y + k) % NY, 1 - core)]
    partners += [x_dev((x + k) % NX) for k in (2, 1, 3)] + [sibling]
    for dev in partners:
        pl.semaphore_signal(barrier, inc=1, device_id=dev, device_id_type=pl.DeviceIdType.MESH)
    own_cot = xc.at[yhi, core, ylo, x, 1]
    loads = {}
    for i, (src, dst) in enumerate((
        (tok_hbm, tok_ref), (cot_hbm, own_cot), (job_hbm, job_ref), (a_hbm, a_ref),
        (gut_hbm, gut_ref), (dn_hbm, dn_ref), (bt_hbm, bt_ref),
    )):
        loads[i] = pltpu.make_async_copy(src, dst, load_s.at[i])
        loads[i].start()
    stores = []

    def store(i, src, dst):
        copy = pltpu.make_async_copy(src, dst, store_s.at[i])
        copy.start()
        stores.append(copy)

    eye = (
        lax.broadcasted_iota(jnp.int32, (256, 256), 0)
        == lax.broadcasted_iota(jnp.int32, (256, 256), 1)
    ).astype(F32).astype(BF16)

    def turned(ref):
        cols = ref.shape[1]
        return jnp.concatenate(
            [mm_nt(eye, ref[:, i:i + 256]) for i in range(0, cols, 256)], axis=0
        ).astype(BF16)

    loads[0].wait()
    xc[yhi, core, :, :, 0] = turned(tok_ref).reshape(NYLO, NX, PIECE, JOB_ROWS)
    loads[1].wait()
    loads[2].wait()
    jobs[yhi, core] = jnp.broadcast_to(job_ref[...].astype(F32), (16, JOB_ROWS)).astype(BF16)
    pl.semaphore_wait(barrier, len(partners))

    def piece(k, src, low, at_x):
        view = xc.at[src, core, low, at_x]
        return view if k else xc.at[src, core, low, at_x, 1]

    both_low = pl.ds(0, NYLO)
    order = (0, 1, 3, 2)
    source = [(yhi + NYHI - k) % NYHI for k in range(NYHI)]
    own = xc.at[yhi, core, ylo, x]
    send(own_cot, own_cot, ty_s.at[0, 0], ty_r.at[0, 0], y_dev(yhi * NYLO + 1 - ylo))
    for k in order[1:]:
        for low in range(NYLO):
            dev = y_dev(((yhi + k) % NYHI) * NYLO + low)
            send(own, own, ty_s.at[k, low], ty_r.at[k, ylo], dev)
    own = xc.at[yhi, core, :, :, 0]
    send(own, own, tc_s.at[NYHI], tc_r.at[NYHI], sibling)
    own = jobs.at[yhi, core]
    for k in range(1, NYHI):
        dev = y_dev(((yhi + k) % NYHI) * NYLO + ylo)
        send(own, own, jy_s.at[k - 1], jy_r.at[k - 1], dev)
    loads[3].wait()
    for k in range(2):
        at[k * JOB_COLS:(k + 1) * JOB_COLS, :] = turned(a_ref.at[k])
    x_next = (x_dev((x + 1) % NX), x_dev((x + NX - 1) % NX))
    x_from = ((x + NX - 1) % NX, (x + 1) % NX)
    for k in order:
        src = source[k]
        if k == 0:
            arrived(piece(0, src, 1 - ylo, x), ty_s.at[0, 0], ty_r.at[0, 0])
        else:
            for low in range(NYLO):
                arrived(piece(k, src, low, x), ty_s.at[k, low], ty_r.at[k, low])
        for way in range(2):
            own = piece(k, src, both_low, x)
            send(own, own, tx_s.at[k, way], tx_r.at[k, way], x_next[way])
    for k in range(1, NYHI):
        arrived(jobs.at[source[k], core], jy_s.at[k - 1], jy_r.at[k - 1])
    send(jobs.at[:, core], jobs.at[:, core], jc_s.at[0], jc_r.at[0], sibling)
    for i in range(4, 7):
        loads[i].wait()
    for k in range(2):
        gu[k] = turned(gut_ref.at[k])
        bn[k] = turned(bt_ref.at[k])
    dnt[...] = turned(dn_ref)
    for k in order:
        for way in range(2):
            arrived(piece(k, source[k], both_low, x_from[way]), tx_s.at[k, way], tx_r.at[k, way])
            onward = piece(k, source[k], way, x_from[way])
            send(onward, onward, tf_s.at[k, way], tf_r.at[k, way], x_next[way])
    for k in order:
        for way in range(2):
            across = piece(k, source[k], way, (x + 2) % NX)
            arrived(across, tf_s.at[k, way], tf_r.at[k, way])
        whole = xc.at[source[k], core] if k else xc.at[yhi, core, :, :, 1]
        send(whole, whole, tc_s.at[k], tc_r.at[k], sibling)
    arrived(jobs.at[:, 1 - core], jc_s.at[0], jc_r.at[0])
    arrived(xc.at[yhi, 1 - core, :, :, 0], tc_s.at[NYHI], tc_r.at[NYHI])
    for k in order:
        whole = xc.at[source[k], 1 - core] if k else xc.at[yhi, 1 - core, :, :, 1]
        arrived(whole, tc_s.at[k], tc_r.at[k])

    def wide_mask(row):
        row = row.astype(F32)[0:1]
        col = lax.broadcasted_iota(jnp.int32, (JOB_COLS, row.shape[1]), 0) // ADAPTER_RANK
        return col.astype(F32) == row

    def pair(kind, q):
        return jnp.concatenate(
            [xc[q, c, :, :, kind].reshape(FEAT, JOB_ROWS) for c in range(NCORE)], axis=1
        )

    def pair_mask(q):
        return wide_mask(jnp.concatenate([jobs[q, c] for c in range(NCORE)], axis=1))

    def forward_sums(q):
        rows = pair(0, q)
        mask = pair_mask(q)
        pre = [mm(gut_ref[k], rows) for k in range(2)]
        low = mm(at[...], rows)
        for k in range(2):
            picked = jnp.where(mask, low[k * JOB_COLS:(k + 1) * JOB_COLS], 0.0)
            picked = picked.reshape(JOB_COUNT, ADAPTER_RANK, 2 * JOB_ROWS).sum(0)
            low_at = LOW_AT + k * ADAPTER_RANK
            for c in range(NCORE):
                cut = slice(c * JOB_ROWS, (c + 1) * JOB_ROWS)
                part[NCORE * q + c, k * HID:(k + 1) * HID, :] = pre[k][:, cut]
                part[NCORE * q + c, low_at:low_at + ADAPTER_RANK, :] = picked[:, cut]

    def backward_sums(q):
        back = mm(dn_ref[...], pair(1, q))
        for c in range(NCORE):
            part[NCORE * q + c, BACK_AT:, :] = back[:, c * JOB_ROWS:(c + 1) * JOB_ROWS]

    def sum_step(t, chunks):
        ready = []
        for way in range(2):
            cuts = [c for c in chunks if t > 0 or c % 2 == way]
            cuts.sort(key=lambda c: (c // 2 if t > 1 else 0, c % 2 == way))
            ready.append(cuts)
        for cuts in zip(*ready):
            for way, c in enumerate(cuts):
                block = (z + 4 - t) % NZ if way == 0 else (z + 4 + t) % NZ
                lo, hi = SUMS[c]
                value = part[block, lo:hi, :]
                if t > 1 or (t == 1 and c % 2 == way):
                    before = ring_in.at[way, t - 1, lo:hi]
                    arrived(before, rs_s.at[way, t - 1, c], rs_r.at[way, t - 1, c])
                    value = value + before[...].astype(F32)
                ring_out[way, t, lo:hi, :] = value.astype(BF16)
                send(ring_out.at[way, t, lo:hi], ring_in.at[way, t, lo:hi],
                     rs_s.at[way, t, c], rs_r.at[way, t, c], next_dev[way])

    def sum_end(chunks):
        for c in chunks:
            lo, hi = SUMS[c]
            for way in range(2):
                arrived(ring_in.at[way, 3, lo:hi], rs_s.at[way, 3, c], rs_r.at[way, 3, c])
        lo, hi = SUMS[chunks[0]][0], SUMS[chunks[-1]][1]
        return part[z, lo:hi, :] + (
            ring_in[0, 3, lo:hi, :].astype(F32) + ring_in[1, 3, lo:hi, :].astype(F32)
        )

    def gather_step(t, chunks):
        for c in chunks:
            lo, hi = PARTS[c]
            for way in range(2):
                block = (z + NZ - t) % NZ if way == 0 else (z + t) % NZ
                piece = held.at[block, lo:hi]
                if t > 0:
                    arrived(piece, zg_s.at[way, t - 1, c], zg_r.at[way, t - 1, c])
                if t < 3 or c % 2 == way:
                    send(piece, piece, zg_s.at[way, t, c], zg_r.at[way, t, c], next_dev[way])

    def gather_end(chunks):
        for c in chunks:
            lo, hi = PARTS[c]
            arrived(held.at[far, lo:hi], zg_s.at[c % 2, 3, c], zg_r.at[c % 2, 3, c])

    def blocks_at(t):
        if t == 0 or t == 4:
            return [(z + t) % NZ]
        return [(z + NZ - t) % NZ, (z + t) % NZ]

    def held_rows(blocks, lo, hi):
        return jnp.concatenate([held[p, lo:hi, :] for p in blocks], axis=1)

    def slots(t):
        first = (0, 1, 3, 5, 7)[t]
        return [(first + i, p) for i, p in enumerate(blocks_at(t))]

    def core_stage(t):
        blocks = blocks_at(t)
        values = (
            mm(dnt[...], held_rows(blocks, 0, HID)),
            mm(gu[0], held_rows(blocks, GRAD_AT, GRAD_AT + HID))
            + mm(gu[1], held_rows(blocks, GRAD_AT + HID, ROWS)),
        )
        for j, (n, _) in enumerate(slots(t)):
            for i in range(2):
                cut = values[i][:, j * JOB_ROWS:(j + 1) * JOB_ROWS].astype(BF16)
                outp[n, i] = cut.reshape(NYLO, NX, PIECE, JOB_ROWS)
            send(outp.at[n, 1 - core], core_in.at[n], oc_s.at[n], oc_r.at[n], sibling)

    def x_stage(t):
        for n, _ in slots(t):
            arrived(core_in.at[n], oc_s.at[n], oc_r.at[n])
            x_out[n] = (outp[n, core].astype(F32) + core_in[n].astype(F32)).astype(BF16)
            for k in range(1, NX):
                other = (x + k) % NX
                send(x_out.at[n, :, other], x_in.at[n, k - 1],
                     ox_s.at[n, k - 1], ox_r.at[n, k - 1], x_dev(other))

    def y_copies(n, p):
        for low in range(NYLO):
            other = (p // NCORE) * NYLO + low
            k = (other + NY - y) % NY
            here = (p == dp) & (low == ylo)
            yield low, here, pltpu.make_async_remote_copy(
                src_ref=y_out.at[n, low], dst_ref=y_in.at[core, k],
                send_sem=oy_s.at[n, low], recv_sem=oy_r.at[core, k],
                device_id=final_dev(other, p % NCORE), device_id_type=pl.DeviceIdType.MESH,
            )

    def y_stage(t):
        for n, p in slots(t):
            both = x_out[n, :, x].astype(F32)
            for k in range(1, NX):
                arrived(x_in.at[n, k - 1], ox_s.at[n, k - 1], ox_r.at[n, k - 1])
                both = both + x_in[n, k - 1].astype(F32)
            y_out[n] = both.astype(BF16)
            for low, here, copy in y_copies(n, p):
                @pl.when(jnp.logical_not(here))
                def _(copy=copy):
                    copy.start()

                @pl.when(here)
                def _(n=n, low=low):
                    fin[...] = y_out[n, low].astype(F32)

    def y_settle(t):
        for n, p in slots(t):
            for _, here, copy in y_copies(n, p):
                @pl.when(jnp.logical_not(here))
                def _(copy=copy):
                    copy.wait_send()

    forward, backward = (0, 1), (2, 3)
    every = forward + backward
    forward_sums(far // NCORE)
    backward_sums(far // NCORE)
    sum_step(0, every)

    @pl.loop(1, NYHI)
    def _(q):
        forward_sums((far // NCORE + q) % NYHI)
        backward_sums((far // NCORE + q) % NYHI)

    for t in range(1, 4):
        sum_step(t, every)

    total = sum_end(forward)
    mask = wide_mask(jobs[z // NCORE, z % NCORE])
    pre_act = []
    for k in range(2):
        low = total[LOW_AT + k * ADAPTER_RANK:LOW_AT + (k + 1) * ADAPTER_RANK]
        wide = jnp.where(mask, jnp.concatenate([low] * JOB_COUNT, axis=0), 0.0).astype(BF16)
        pre_act.append(total[k * HID:(k + 1) * HID] + SCALE * mm(bt_ref[k], wide))
    gate, up = pre_act
    sig = jax.nn.sigmoid(gate)
    silu = gate * sig
    held[z, 0:HID, :] = (silu * up).astype(BF16)
    held[z, HLOW_AT:GRAD_AT, :] = total[LOW_AT:BACK_AT].astype(BF16)
    gather_step(0, forward)
    back = sum_end(backward)
    grads = [
        (back * up * sig * (1.0 + gate * (1.0 - sig))).astype(BF16),
        (back * silu).astype(BF16),
    ]
    for k in range(2):
        held[z, GRAD_AT + k * HID:GRAD_AT + (k + 1) * HID, :] = grads[k]
    gather_step(0, backward)
    for k in range(2):
        wide = jnp.where(mask, mm(bn[k], grads[k]), 0.0)
        b_core_out[k * ADAPTER_RANK:(k + 1) * ADAPTER_RANK, :] = SCALE * wide.reshape(
            JOB_COUNT, ADAPTER_RANK, JOB_ROWS
        ).sum(0)
    send(b_core_out, b_core_in, bc_s.at[0], bc_r.at[0], sibling)
    core_stage(0)
    arrived(b_core_in, bc_s.at[0], bc_r.at[0])
    b_x_out[...] = b_core_out[...] + b_core_in[...]
    for k in range(1, NX):
        send(b_x_out, b_x_in.at[k - 1], bx_s.at[k - 1], bx_r.at[k - 1], x_dev((x + k) % NX))
    gather_step(1, every)
    core_stage(1)
    x_stage(0)
    x_stage(1)
    both = b_x_out[...]
    for k in range(1, NX):
        arrived(b_x_in.at[k - 1], bx_s.at[k - 1], bx_r.at[k - 1])
        both = both + b_x_in[k - 1]
    b_y_out[...] = both
    for k in range(1, NY):
        send(b_y_out, b_y_in.at[k - 1], by_s.at[k - 1], by_r.at[k - 1], y_dev((y + k) % NY))
    gather_step(2, every)
    core_stage(2)
    y_stage(0)
    x_stage(2)
    gather_step(3, every)
    core_stage(3)
    y_stage(1)
    x_stage(3)
    both = b_y_out[...]
    for k in range(1, NY):
        arrived(b_y_in.at[k - 1], by_s.at[k - 1], by_r.at[k - 1])
        both = both + b_y_in[k - 1]
    inner[z] = both
    for k in range(1, NZ):
        send(inner.at[z], inner.at[z], bz_s.at[k - 1], bz_r.at[k - 1], z_dev((z + k) % NZ))
    gather_end(every)
    core_stage(4)
    y_stage(2)
    x_stage(4)
    for k in range(2):
        acc = jnp.zeros((HID, JOB_COLS), F32)
        for q in range(NYHI):
            blocks = [NCORE * q + c for c in range(NCORE)]
            low_at, grad_at = HLOW_AT + k * ADAPTER_RANK, GRAD_AT + k * HID
            low = held_rows(blocks, low_at, low_at + ADAPTER_RANK).astype(F32)
            wide = jnp.where(pair_mask(q), jnp.concatenate([low] * JOB_COUNT, axis=0), 0.0)
            acc = acc + mm_nt(held_rows(blocks, grad_at, grad_at + HID), wide.astype(BF16))
        gb_ref[k] = SCALE * acc
    store(3, gb_ref, gb_hbm)
    y_stage(3)
    y_stage(4)
    for k in range(1, NZ):
        arrived(inner.at[(z + NZ - k) % NZ], bz_s.at[k - 1], bz_r.at[k - 1])

    def wide_inner(k, blocks, mask):
        rows = [inner[p, k * ADAPTER_RANK:(k + 1) * ADAPTER_RANK, :] for p in blocks]
        rows = jnp.concatenate(rows, axis=1)
        wide = jnp.where(mask, jnp.concatenate([rows] * JOB_COUNT, axis=0), 0.0)
        hi = wide.astype(BF16)
        return hi, (wide - hi.astype(F32)).astype(BF16)

    for k in range(2):
        acc = jnp.zeros((FEAT, JOB_COLS), F32)
        for q in range(NYHI):
            rows = pair(0, q)
            for wide in wide_inner(k, [NCORE * q + c for c in range(NCORE)], pair_mask(q)):
                acc = acc + mm_nt(rows, wide)
        ga_ref[k] = acc
    store(2, ga_ref, ga_hbm)
    mask = wide_mask(jobs[yhi, core])
    extra = jnp.zeros((PIECE, JOB_ROWS), F32)
    for k in range(2):
        cols = a_ref[k, pl.ds(pl.multiple_of(hid * PIECE, PIECE), PIECE), :]
        for wide in wide_inner(k, [dp], mask):
            extra = extra + mm(cols, wide)
    for copy in sent:
        copy.wait_send()
    for t in range(4):
        y_settle(t)
    sums = []
    for c in range(NCORE):
        both = jnp.zeros((PIECE, JOB_ROWS), F32)
        for k in range(1, NY):
            arrived(y_in.at[c, k], oy_s.at[0, 0], oy_r.at[c, k])
            both = both + y_in[c, k].astype(F32)
        sums.append(both)
    arrived(y_in.at[1 - core, 0], oy_s.at[0, 0], oy_r.at[1 - core, 0])
    near = y_in[1 - core, 0].astype(F32)
    mixed_ref[...] = (sums[0] + jnp.where(core == 0, fin[...], near)).astype(BF16)
    ig_ref[...] = (sums[1] + extra + jnp.where(core == 0, near, fin[...])).astype(BF16)
    store(0, mixed_ref, mixed_hbm)
    store(1, ig_ref, ig_hbm)
    y_settle(4)
    for copy in stores:
        copy.wait()


def hand_over(*refs):
    srcs, dsts, held = refs[0:4], refs[4:8], refs[8:12]
    load_sem, store_sem = refs[12:14]
    cuts = [(i, ()) for i in range(2)] + [
        (i, (k, pl.ds(j * rows, rows))) for i, rows in ((2, 256), (3, 112))
        for k in range(2) for j in range(2)
    ]
    loads, stores = [], []
    for n, (i, cut) in enumerate(cuts):
        src, own, dst = (ref.at[cut] if cut else ref for ref in (srcs[i], held[i], dsts[i]))
        loads.append(pltpu.make_async_copy(src, own, load_sem.at[n]))
        stores.append(pltpu.make_async_copy(own, dst, store_sem.at[n]))
        loads[-1].start()
    for load, copy in zip(loads, stores):
        load.wait()
        copy.start()
    for copy in stores:
        copy.wait()


def local(tokens, token_job_index, gate_up, down, adapter_in, adapter_out, cotangent):
    hbm = pl.BlockSpec(memory_space=pltpu.HBM)
    buf = pltpu.VMEM
    tile = (PIECE, JOB_ROWS)
    ring = (2, 4, 4)
    sems = [
        (NYHI, NYLO), (NYHI, 2), (NYHI, 2), (NYHI + 1,), (NYHI - 1,), (1,),
        ring, ring, (NZ,), (NZ, NX - 1), None,
        (1,), (NX - 1,), (NY - 1,), (NZ - 1,),
    ]
    sems = [(s, s) if s else ((NZ, NYLO), (NCORE, NY)) for s in sems]
    outs = pl.pallas_call(
        kernel,
        out_shape=[
            jax.ShapeDtypeStruct(tile, BF16),
            jax.ShapeDtypeStruct(tile, BF16),
            jax.ShapeDtypeStruct((2, FEAT, JOB_COLS), F32),
            jax.ShapeDtypeStruct((2, HID, JOB_COLS), F32),
        ],
        in_specs=[hbm] * 7,
        out_specs=[hbm] * 4,
        scratch_shapes=[
            buf((JOB_ROWS, FEAT), BF16),
            buf((1, JOB_ROWS), jnp.int32),
            buf((2, HID, FEAT), BF16),
            buf((HID, FEAT), BF16),
            buf((2, FEAT, JOB_COLS), BF16),
            buf((2, HID, JOB_COLS), BF16),
            buf(tile, BF16),
            buf(tile, BF16),
            buf((2, FEAT, JOB_COLS), F32),
            buf((2, HID, JOB_COLS), F32),
            buf((NYHI, NCORE, NYLO, NX, 2) + tile, BF16),
            buf((NYHI, NCORE, 16, JOB_ROWS), BF16),
            buf((2, FEAT, HID), BF16),
            buf((FEAT, HID), BF16),
            buf((2 * JOB_COLS, FEAT), BF16),
            buf((2, JOB_COLS, HID), BF16),
            buf((NZ, ROWS, JOB_ROWS), F32),
            buf((2, 4, ROWS, JOB_ROWS), BF16),
            buf((2, 4, ROWS, JOB_ROWS), BF16),
            buf((NZ, ROWS, JOB_ROWS), BF16),
            buf((NZ, 2, NYLO, NX) + tile, BF16),
            buf((NZ, NYLO, NX) + tile, BF16),
            buf((NZ, NYLO, NX) + tile, BF16),
            buf((NZ, NX - 1, NYLO) + tile, BF16),
            buf((NZ, NYLO) + tile, BF16),
            buf((NCORE, NY) + tile, BF16),
            buf(tile, F32),
            buf((LOW, JOB_ROWS), F32),
            buf((LOW, JOB_ROWS), F32),
            buf((LOW, JOB_ROWS), F32),
            buf((NX - 1, LOW, JOB_ROWS), F32),
            buf((LOW, JOB_ROWS), F32),
            buf((NY - 1, LOW, JOB_ROWS), F32),
            buf((NZ, LOW, JOB_ROWS), F32),
        ] + [pltpu.SemaphoreType.DMA(s) for pair in sems for s in pair] + [
            pltpu.SemaphoreType.DMA((7,)), pltpu.SemaphoreType.DMA((4,)),
        ],
        compiler_params=pltpu.CompilerParams(
            collective_id=0, has_side_effects=True, vmem_limit_bytes=63 * 1024 * 1024
        ),
    )(
        tokens, token_job_index.reshape(1, JOB_ROWS), jnp.swapaxes(gate_up, 1, 2), down,
        adapter_in, jnp.swapaxes(adapter_out, 1, 2), cotangent.T,
    )
    dma = pltpu.SemaphoreType.DMA((10,))
    mixed, grad, grad_in, grad_out = pl.pallas_call(
        hand_over,
        out_shape=[jax.ShapeDtypeStruct(out.shape, out.dtype) for out in outs],
        in_specs=[hbm] * 4,
        out_specs=[hbm] * 4,
        scratch_shapes=[buf(out.shape, out.dtype) for out in outs] + [dma, dma],
        compiler_params=pltpu.CompilerParams(vmem_limit_bytes=63 * 1024 * 1024),
    )(*outs)
    return mixed.T, grad.T, grad_in, jnp.swapaxes(grad_out, 1, 2)


def solution(mesh):
    return jax.shard_map(
        local,
        mesh=mesh,
        in_specs=(
            P("dp", "width"),
            P("dp"),
            P(None, "width", ("dp", "hidden")),
            P(("dp", "hidden"), "width"),
            P(None, "width", None),
            P(None, None, ("dp", "hidden")),
            P("dp", ("width", "hidden")),
        ),
        out_specs=(
            P("dp", ("width", "hidden")),
            P("dp", ("width", "hidden")),
            P(None, "width", None),
            P(None, None, ("dp", "hidden")),
        ),
        check_vma=False,
    )
```

```python
import jax
import jax.numpy as jnp
from jax import lax
from jax.experimental import pallas as pl
from jax.experimental.pallas import tpu as pltpu
from jax.sharding import PartitionSpec as P

JOB_COUNT = 16
ADAPTER_RANK = 16
JOB_COLS = JOB_COUNT * ADAPTER_RANK
JOB_ROWS = 128
SCALE = 0.5
F32 = jnp.float32
BF16 = jnp.bfloat16

NX, NYLO, NYHI, NCORE, NZ = 4, 2, 4, 2, 8
NY = NYLO * NYHI
PIECE = 64
FEAT = NX * NYLO * PIECE
HID = 224
LOW = 2 * ADAPTER_RANK
SUMS = ((0, 240), (240, 480), (480, 592), (592, 704))
LOW_AT, BACK_AT = 2 * HID, 2 * HID + LOW
PARTS = ((0, 128), (128, 256), (256, 480), (480, 704))
HLOW_AT, GRAD_AT = HID, HID + LOW
ROWS = 3 * HID + LOW


def mm(a, b):
    return jnp.dot(a, b, preferred_element_type=F32)


def mm_nt(a, b):
    return lax.dot_general(a, b, (((1,), (1,)), ((), ())), preferred_element_type=F32)


def kernel(
    tok_hbm, job_hbm, gut_hbm, dn_hbm, a_hbm, bt_hbm, cot_hbm,
    mixed_hbm, ig_hbm, ga_hbm, gb_hbm,
    tok_ref, job_ref, gut_ref, dn_ref, a_ref, bt_ref,
    mixed_ref, ig_ref, ga_ref, gb_ref,
    xc, jobs, gu, dnt, at, bn,
    part, ring_out, ring_in, held,
    outp, core_in, x_out, x_in, y_out, y_in, fin,
    b_core_out, b_core_in, b_x_out, b_x_in, b_y_out, b_y_in, inner,
    ty_s, ty_r, tx_s, tx_r, tf_s, tf_r, tc_s, tc_r, jy_s, jy_r, jc_s, jc_r,
    rs_s, rs_r, zg_s, zg_r, oc_s, oc_r, ox_s, ox_r, oy_s, oy_r,
    bc_s, bc_r, bx_s, bx_r, by_s, by_r, bz_s, bz_r, load_s, store_s,
):
    dp = lax.axis_index("dp")
    z = lax.axis_index("width")
    hid = lax.axis_index("hidden")
    yhi, core = dp // NCORE, dp % NCORE
    ylo, x = hid // NX, hid % NX
    y = yhi * NYLO + ylo
    sibling = (yhi * NCORE + 1 - core, z, hid)
    far = (z + NZ // 2) % NZ

    def y_dev(other):
        return ((other // NYLO) * NCORE + core, z, (other % NYLO) * NX + x)

    def final_dev(other, other_core):
        return ((other // NYLO) * NCORE + other_core, z, (other % NYLO) * NX + x)

    def x_dev(other):
        return (dp, z, ylo * NX + other)

    def z_dev(other):
        return (dp, other, hid)

    next_dev = (z_dev((z + 1) % NZ), z_dev((z + NZ - 1) % NZ))
    sent = []

    def send(src, dst, s, r, dev):
        copy = pltpu.make_async_remote_copy(
            src_ref=src, dst_ref=dst, send_sem=s, recv_sem=r,
            device_id=dev, device_id_type=pl.DeviceIdType.MESH,
        )
        copy.start()
        sent.append(copy)

    def arrived(dst, s, r):
        pltpu.make_async_remote_copy(
            src_ref=dst, dst_ref=dst, send_sem=s, recv_sem=r,
            device_id=sibling, device_id_type=pl.DeviceIdType.MESH,
        ).wait_recv()

    barrier = pltpu.get_barrier_semaphore()
    far_first = (4, 3, 5, 2, 6, 1, 7)
    partners = [z_dev((z + k) % NZ) for k in far_first]
    for k in far_first:
        partners += [y_dev((y + k) % NY), final_dev((y + k) % NY, 1 - core)]
    partners += [x_dev((x + k) % NX) for k in (2, 1, 3)] + [sibling]
    for dev in partners:
        pl.semaphore_signal(barrier, inc=1, device_id=dev, device_id_type=pl.DeviceIdType.MESH)
    own_cot = xc.at[yhi, core, ylo, x, 1]
    loads = {}
    for i, (src, dst) in enumerate((
        (tok_hbm, tok_ref), (cot_hbm, own_cot), (job_hbm, job_ref), (a_hbm, a_ref),
        (gut_hbm, gut_ref), (dn_hbm, dn_ref), (bt_hbm, bt_ref),
    )):
        loads[i] = pltpu.make_async_copy(src, dst, load_s.at[i])
        loads[i].start()
    stores = []

    def store(i, src, dst):
        copy = pltpu.make_async_copy(src, dst, store_s.at[i])
        copy.start()
        stores.append(copy)

    eye = (
        lax.broadcasted_iota(jnp.int32, (256, 256), 0)
        == lax.broadcasted_iota(jnp.int32, (256, 256), 1)
    ).astype(F32).astype(BF16)

    def turned(ref):
        cols = ref.shape[1]
        return jnp.concatenate(
            [mm_nt(eye, ref[:, i:i + 256]) for i in range(0, cols, 256)], axis=0
        ).astype(BF16)

    loads[0].wait()
    xc[yhi, core, :, :, 0] = turned(tok_ref).reshape(NYLO, NX, PIECE, JOB_ROWS)
    loads[1].wait()
    loads[2].wait()
    jobs[yhi, core] = jnp.broadcast_to(job_ref[...].astype(F32), (16, JOB_ROWS)).astype(BF16)
    pl.semaphore_wait(barrier, len(partners))

    def piece(k, src, low, at_x):
        view = xc.at[src, core, low, at_x]
        return view if k else xc.at[src, core, low, at_x, 1]

    both_low = pl.ds(0, NYLO)
    order = (0, 1, 3, 2)
    source = [(yhi + NYHI - k) % NYHI for k in range(NYHI)]
    own = xc.at[yhi, core, ylo, x]
    send(own_cot, own_cot, ty_s.at[0, 0], ty_r.at[0, 0], y_dev(yhi * NYLO + 1 - ylo))
    for k in order[1:]:
        for low in range(NYLO):
            dev = y_dev(((yhi + k) % NYHI) * NYLO + low)
            send(own, own, ty_s.at[k, low], ty_r.at[k, ylo], dev)
    own = xc.at[yhi, core, :, :, 0]
    send(own, own, tc_s.at[NYHI], tc_r.at[NYHI], sibling)
    own = jobs.at[yhi, core]
    for k in range(1, NYHI):
        dev = y_dev(((yhi + k) % NYHI) * NYLO + ylo)
        send(own, own, jy_s.at[k - 1], jy_r.at[k - 1], dev)
    loads[3].wait()
    for k in range(2):
        at[k * JOB_COLS:(k + 1) * JOB_COLS, :] = turned(a_ref.at[k])
    x_next = (x_dev((x + 1) % NX), x_dev((x + NX - 1) % NX))
    x_from = ((x + NX - 1) % NX, (x + 1) % NX)
    for k in order:
        src = source[k]
        if k == 0:
            arrived(piece(0, src, 1 - ylo, x), ty_s.at[0, 0], ty_r.at[0, 0])
        else:
            for low in range(NYLO):
                arrived(piece(k, src, low, x), ty_s.at[k, low], ty_r.at[k, low])
        for way in range(2):
            own = piece(k, src, both_low, x)
            send(own, own, tx_s.at[k, way], tx_r.at[k, way], x_next[way])
    for k in range(1, NYHI):
        arrived(jobs.at[source[k], core], jy_s.at[k - 1], jy_r.at[k - 1])
    send(jobs.at[:, core], jobs.at[:, core], jc_s.at[0], jc_r.at[0], sibling)
    for i in range(4, 7):
        loads[i].wait()
    for k in range(2):
        gu[k] = turned(gut_ref.at[k])
        bn[k] = turned(bt_ref.at[k])
    dnt[...] = turned(dn_ref)
    for k in order:
        for way in range(2):
            arrived(piece(k, source[k], both_low, x_from[way]), tx_s.at[k, way], tx_r.at[k, way])
            onward = piece(k, source[k], way, x_from[way])
            send(onward, onward, tf_s.at[k, way], tf_r.at[k, way], x_next[way])
    for k in order:
        for way in range(2):
            across = piece(k, source[k], way, (x + 2) % NX)
            arrived(across, tf_s.at[k, way], tf_r.at[k, way])
        whole = xc.at[source[k], core] if k else xc.at[yhi, core, :, :, 1]
        send(whole, whole, tc_s.at[k], tc_r.at[k], sibling)
    arrived(jobs.at[:, 1 - core], jc_s.at[0], jc_r.at[0])
    arrived(xc.at[yhi, 1 - core, :, :, 0], tc_s.at[NYHI], tc_r.at[NYHI])
    for k in order:
        whole = xc.at[source[k], 1 - core] if k else xc.at[yhi, 1 - core, :, :, 1]
        arrived(whole, tc_s.at[k], tc_r.at[k])

    def wide_mask(row):
        row = row.astype(F32)[0:1]
        col = lax.broadcasted_iota(jnp.int32, (JOB_COLS, row.shape[1]), 0) // ADAPTER_RANK
        return col.astype(F32) == row

    def pair(kind, q):
        return jnp.concatenate(
            [xc[q, c, :, :, kind].reshape(FEAT, JOB_ROWS) for c in range(NCORE)], axis=1
        )

    def pair_mask(q):
        return wide_mask(jnp.concatenate([jobs[q, c] for c in range(NCORE)], axis=1))

    def forward_sums(q):
        rows = pair(0, q)
        mask = pair_mask(q)
        pre = [mm(gut_ref[k], rows) for k in range(2)]
        low = mm(at[...], rows)
        for k in range(2):
            picked = jnp.where(mask, low[k * JOB_COLS:(k + 1) * JOB_COLS], 0.0)
            picked = picked.reshape(JOB_COUNT, ADAPTER_RANK, 2 * JOB_ROWS).sum(0)
            low_at = LOW_AT + k * ADAPTER_RANK
            for c in range(NCORE):
                cut = slice(c * JOB_ROWS, (c + 1) * JOB_ROWS)
                part[NCORE * q + c, k * HID:(k + 1) * HID, :] = pre[k][:, cut]
                part[NCORE * q + c, low_at:low_at + ADAPTER_RANK, :] = picked[:, cut]

    def backward_sums(q):
        back = mm(dn_ref[...], pair(1, q))
        for c in range(NCORE):
            part[NCORE * q + c, BACK_AT:, :] = back[:, c * JOB_ROWS:(c + 1) * JOB_ROWS]

    def sum_step(t, chunks):
        ready = []
        for way in range(2):
            cuts = [c for c in chunks if t > 0 or c % 2 == way]
            cuts.sort(key=lambda c: (c // 2 if t > 1 else 0, c % 2 == way))
            ready.append(cuts)
        for cuts in zip(*ready):
            for way, c in enumerate(cuts):
                block = (z + 4 - t) % NZ if way == 0 else (z + 4 + t) % NZ
                lo, hi = SUMS[c]
                value = part[block, lo:hi, :]
                if t > 1 or (t == 1 and c % 2 == way):
                    before = ring_in.at[way, t - 1, lo:hi]
                    arrived(before, rs_s.at[way, t - 1, c], rs_r.at[way, t - 1, c])
                    value = value + before[...].astype(F32)
                ring_out[way, t, lo:hi, :] = value.astype(BF16)
                send(ring_out.at[way, t, lo:hi], ring_in.at[way, t, lo:hi],
                     rs_s.at[way, t, c], rs_r.at[way, t, c], next_dev[way])

    def sum_end(chunks):
        for c in chunks:
            lo, hi = SUMS[c]
            for way in range(2):
                arrived(ring_in.at[way, 3, lo:hi], rs_s.at[way, 3, c], rs_r.at[way, 3, c])
        lo, hi = SUMS[chunks[0]][0], SUMS[chunks[-1]][1]
        return part[z, lo:hi, :] + (
            ring_in[0, 3, lo:hi, :].astype(F32) + ring_in[1, 3, lo:hi, :].astype(F32)
        )

    def gather_step(t, chunks):
        for c in chunks:
            lo, hi = PARTS[c]
            for way in range(2):
                block = (z + NZ - t) % NZ if way == 0 else (z + t) % NZ
                piece = held.at[block, lo:hi]
                if t > 0:
                    arrived(piece, zg_s.at[way, t - 1, c], zg_r.at[way, t - 1, c])
                if t < 3 or c % 2 == way:
                    send(piece, piece, zg_s.at[way, t, c], zg_r.at[way, t, c], next_dev[way])

    def gather_end(chunks):
        for c in chunks:
            lo, hi = PARTS[c]
            arrived(held.at[far, lo:hi], zg_s.at[c % 2, 3, c], zg_r.at[c % 2, 3, c])

    def blocks_at(t):
        if t == 0 or t == 4:
            return [(z + t) % NZ]
        return [(z + NZ - t) % NZ, (z + t) % NZ]

    def held_rows(blocks, lo, hi):
        return jnp.concatenate([held[p, lo:hi, :] for p in blocks], axis=1)

    def slots(t):
        first = (0, 1, 3, 5, 7)[t]
        return [(first + i, p) for i, p in enumerate(blocks_at(t))]

    def core_stage(t):
        blocks = blocks_at(t)
        values = (
            mm(dnt[...], held_rows(blocks, 0, HID)),
            mm(gu[0], held_rows(blocks, GRAD_AT, GRAD_AT + HID))
            + mm(gu[1], held_rows(blocks, GRAD_AT + HID, ROWS)),
        )
        for j, (n, _) in enumerate(slots(t)):
            for i in range(2):
                cut = values[i][:, j * JOB_ROWS:(j + 1) * JOB_ROWS].astype(BF16)
                outp[n, i] = cut.reshape(NYLO, NX, PIECE, JOB_ROWS)
            send(outp.at[n, 1 - core], core_in.at[n], oc_s.at[n], oc_r.at[n], sibling)

    def x_stage(t):
        for n, _ in slots(t):
            arrived(core_in.at[n], oc_s.at[n], oc_r.at[n])
            x_out[n] = (outp[n, core].astype(F32) + core_in[n].astype(F32)).astype(BF16)
            for k in range(1, NX):
                other = (x + k) % NX
                send(x_out.at[n, :, other], x_in.at[n, k - 1],
                     ox_s.at[n, k - 1], ox_r.at[n, k - 1], x_dev(other))

    def y_copies(n, p):
        for low in range(NYLO):
            other = (p // NCORE) * NYLO + low
            k = (other + NY - y) % NY
            here = (p == dp) & (low == ylo)
            yield low, here, pltpu.make_async_remote_copy(
                src_ref=y_out.at[n, low], dst_ref=y_in.at[core, k],
                send_sem=oy_s.at[n, low], recv_sem=oy_r.at[core, k],
                device_id=final_dev(other, p % NCORE), device_id_type=pl.DeviceIdType.MESH,
            )

    def y_stage(t):
        for n, p in slots(t):
            both = x_out[n, :, x].astype(F32)
            for k in range(1, NX):
                arrived(x_in.at[n, k - 1], ox_s.at[n, k - 1], ox_r.at[n, k - 1])
                both = both + x_in[n, k - 1].astype(F32)
            y_out[n] = both.astype(BF16)
            for low, here, copy in y_copies(n, p):
                @pl.when(jnp.logical_not(here))
                def _(copy=copy):
                    copy.start()

                @pl.when(here)
                def _(n=n, low=low):
                    fin[...] = y_out[n, low].astype(F32)

    def y_settle(t):
        for n, p in slots(t):
            for _, here, copy in y_copies(n, p):
                @pl.when(jnp.logical_not(here))
                def _(copy=copy):
                    copy.wait_send()

    forward, backward = (0, 1), (2, 3)
    every = forward + backward
    forward_sums(far // NCORE)
    backward_sums(far // NCORE)
    sum_step(0, every)

    @pl.loop(1, NYHI)
    def _(q):
        forward_sums((far // NCORE + q) % NYHI)
        backward_sums((far // NCORE + q) % NYHI)

    for t in range(1, 4):
        sum_step(t, every)

    total = sum_end(forward)
    mask = wide_mask(jobs[z // NCORE, z % NCORE])
    pre_act = []
    for k in range(2):
        low = total[LOW_AT + k * ADAPTER_RANK:LOW_AT + (k + 1) * ADAPTER_RANK]
        wide = jnp.where(mask, jnp.concatenate([low] * JOB_COUNT, axis=0), 0.0).astype(BF16)
        pre_act.append(total[k * HID:(k + 1) * HID] + SCALE * mm(bt_ref[k], wide))
    gate, up = pre_act
    sig = jax.nn.sigmoid(gate)
    silu = gate * sig
    held[z, 0:HID, :] = (silu * up).astype(BF16)
    held[z, HLOW_AT:GRAD_AT, :] = total[LOW_AT:BACK_AT].astype(BF16)
    gather_step(0, forward)
    back = sum_end(backward)
    grads = [
        (back * up * sig * (1.0 + gate * (1.0 - sig))).astype(BF16),
        (back * silu).astype(BF16),
    ]
    for k in range(2):
        held[z, GRAD_AT + k * HID:GRAD_AT + (k + 1) * HID, :] = grads[k]
    gather_step(0, backward)
    for k in range(2):
        wide = jnp.where(mask, mm(bn[k], grads[k]), 0.0)
        b_core_out[k * ADAPTER_RANK:(k + 1) * ADAPTER_RANK, :] = SCALE * wide.reshape(
            JOB_COUNT, ADAPTER_RANK, JOB_ROWS
        ).sum(0)
    send(b_core_out, b_core_in, bc_s.at[0], bc_r.at[0], sibling)
    core_stage(0)
    arrived(b_core_in, bc_s.at[0], bc_r.at[0])
    b_x_out[...] = b_core_out[...] + b_core_in[...]
    for k in range(1, NX):
        send(b_x_out, b_x_in.at[k - 1], bx_s.at[k - 1], bx_r.at[k - 1], x_dev((x + k) % NX))
    x_stage(0)
    gather_step(1, every)
    core_stage(1)
    x_stage(1)
    both = b_x_out[...]
    for k in range(1, NX):
        arrived(b_x_in.at[k - 1], bx_s.at[k - 1], bx_r.at[k - 1])
        both = both + b_x_in[k - 1]
    b_y_out[...] = both
    for k in range(1, NY):
        send(b_y_out, b_y_in.at[k - 1], by_s.at[k - 1], by_r.at[k - 1], y_dev((y + k) % NY))
    gather_step(2, every)
    core_stage(2)
    y_stage(0)
    x_stage(2)
    gather_step(3, every)
    core_stage(3)
    y_stage(1)
    x_stage(3)
    both = b_y_out[...]
    for k in range(1, NY):
        arrived(b_y_in.at[k - 1], by_s.at[k - 1], by_r.at[k - 1])
        both = both + b_y_in[k - 1]
    inner[z] = both
    for k in range(1, NZ):
        send(inner.at[z], inner.at[z], bz_s.at[k - 1], bz_r.at[k - 1], z_dev((z + k) % NZ))
    gather_end(every)
    core_stage(4)
    y_stage(2)
    x_stage(4)
    for k in range(2):
        acc = jnp.zeros((HID, JOB_COLS), F32)
        for q in range(NYHI):
            blocks = [NCORE * q + c for c in range(NCORE)]
            low_at, grad_at = HLOW_AT + k * ADAPTER_RANK, GRAD_AT + k * HID
            low = held_rows(blocks, low_at, low_at + ADAPTER_RANK).astype(F32)
            wide = jnp.where(pair_mask(q), jnp.concatenate([low] * JOB_COUNT, axis=0), 0.0)
            acc = acc + mm_nt(held_rows(blocks, grad_at, grad_at + HID), wide.astype(BF16))
        gb_ref[k] = SCALE * acc
    store(3, gb_ref, gb_hbm)
    y_stage(3)
    y_stage(4)
    for k in range(1, NZ):
        arrived(inner.at[(z + NZ - k) % NZ], bz_s.at[k - 1], bz_r.at[k - 1])

    def wide_inner(k, blocks, mask):
        rows = [inner[p, k * ADAPTER_RANK:(k + 1) * ADAPTER_RANK, :] for p in blocks]
        rows = jnp.concatenate(rows, axis=1)
        wide = jnp.where(mask, jnp.concatenate([rows] * JOB_COUNT, axis=0), 0.0)
        hi = wide.astype(BF16)
        return hi, (wide - hi.astype(F32)).astype(BF16)

    for k in range(2):
        acc = jnp.zeros((FEAT, JOB_COLS), F32)
        for q in range(NYHI):
            rows = pair(0, q)
            for wide in wide_inner(k, [NCORE * q + c for c in range(NCORE)], pair_mask(q)):
                acc = acc + mm_nt(rows, wide)
        ga_ref[k] = acc
    store(2, ga_ref, ga_hbm)
    mask = wide_mask(jobs[yhi, core])
    extra = jnp.zeros((PIECE, JOB_ROWS), F32)
    for k in range(2):
        cols = a_ref[k, pl.ds(pl.multiple_of(hid * PIECE, PIECE), PIECE), :]
        for wide in wide_inner(k, [dp], mask):
            extra = extra + mm(cols, wide)
    for copy in sent:
        copy.wait_send()
    for t in range(4):
        y_settle(t)
    sums = []
    for c in range(NCORE):
        both = jnp.zeros((PIECE, JOB_ROWS), F32)
        for k in range(1, NY):
            arrived(y_in.at[c, k], oy_s.at[0, 0], oy_r.at[c, k])
            both = both + y_in[c, k].astype(F32)
        sums.append(both)
    arrived(y_in.at[1 - core, 0], oy_s.at[0, 0], oy_r.at[1 - core, 0])
    near = y_in[1 - core, 0].astype(F32)
    mixed_ref[...] = (sums[0] + jnp.where(core == 0, fin[...], near)).astype(BF16)
    ig_ref[...] = (sums[1] + extra + jnp.where(core == 0, near, fin[...])).astype(BF16)
    store(0, mixed_ref, mixed_hbm)
    store(1, ig_ref, ig_hbm)
    y_settle(4)
    for copy in stores:
        copy.wait()


def hand_over(*refs):
    srcs, dsts, held = refs[0:4], refs[4:8], refs[8:12]
    load_sem, store_sem = refs[12:14]
    cuts = [(i, ()) for i in range(2)] + [
        (i, (k, pl.ds(j * rows, rows))) for i, rows in ((2, 256), (3, 112))
        for k in range(2) for j in range(2)
    ]
    loads, stores = [], []
    for n, (i, cut) in enumerate(cuts):
        src, own, dst = (ref.at[cut] if cut else ref for ref in (srcs[i], held[i], dsts[i]))
        loads.append(pltpu.make_async_copy(src, own, load_sem.at[n]))
        stores.append(pltpu.make_async_copy(own, dst, store_sem.at[n]))
        loads[-1].start()
    for load, copy in zip(loads, stores):
        load.wait()
        copy.start()
    for copy in stores:
        copy.wait()


def local(tokens, token_job_index, gate_up, down, adapter_in, adapter_out, cotangent):
    hbm = pl.BlockSpec(memory_space=pltpu.HBM)
    buf = pltpu.VMEM
    tile = (PIECE, JOB_ROWS)
    ring = (2, 4, 4)
    sems = [
        (NYHI, NYLO), (NYHI, 2), (NYHI, 2), (NYHI + 1,), (NYHI - 1,), (1,),
        ring, ring, (NZ,), (NZ, NX - 1), None,
        (1,), (NX - 1,), (NY - 1,), (NZ - 1,),
    ]
    sems = [(s, s) if s else ((NZ, NYLO), (NCORE, NY)) for s in sems]
    outs = pl.pallas_call(
        kernel,
        out_shape=[
            jax.ShapeDtypeStruct(tile, BF16),
            jax.ShapeDtypeStruct(tile, BF16),
            jax.ShapeDtypeStruct((2, FEAT, JOB_COLS), F32),
            jax.ShapeDtypeStruct((2, HID, JOB_COLS), F32),
        ],
        in_specs=[hbm] * 7,
        out_specs=[hbm] * 4,
        scratch_shapes=[
            buf((JOB_ROWS, FEAT), BF16),
            buf((1, JOB_ROWS), jnp.int32),
            buf((2, HID, FEAT), BF16),
            buf((HID, FEAT), BF16),
            buf((2, FEAT, JOB_COLS), BF16),
            buf((2, HID, JOB_COLS), BF16),
            buf(tile, BF16),
            buf(tile, BF16),
            buf((2, FEAT, JOB_COLS), F32),
            buf((2, HID, JOB_COLS), F32),
            buf((NYHI, NCORE, NYLO, NX, 2) + tile, BF16),
            buf((NYHI, NCORE, 16, JOB_ROWS), BF16),
            buf((2, FEAT, HID), BF16),
            buf((FEAT, HID), BF16),
            buf((2 * JOB_COLS, FEAT), BF16),
            buf((2, JOB_COLS, HID), BF16),
            buf((NZ, ROWS, JOB_ROWS), F32),
            buf((2, 4, ROWS, JOB_ROWS), BF16),
            buf((2, 4, ROWS, JOB_ROWS), BF16),
            buf((NZ, ROWS, JOB_ROWS), BF16),
            buf((NZ, 2, NYLO, NX) + tile, BF16),
            buf((NZ, NYLO, NX) + tile, BF16),
            buf((NZ, NYLO, NX) + tile, BF16),
            buf((NZ, NX - 1, NYLO) + tile, BF16),
            buf((NZ, NYLO) + tile, BF16),
            buf((NCORE, NY) + tile, BF16),
            buf(tile, F32),
            buf((LOW, JOB_ROWS), F32),
            buf((LOW, JOB_ROWS), F32),
            buf((LOW, JOB_ROWS), F32),
            buf((NX - 1, LOW, JOB_ROWS), F32),
            buf((LOW, JOB_ROWS), F32),
            buf((NY - 1, LOW, JOB_ROWS), F32),
            buf((NZ, LOW, JOB_ROWS), F32),
        ] + [pltpu.SemaphoreType.DMA(s) for pair in sems for s in pair] + [
            pltpu.SemaphoreType.DMA((7,)), pltpu.SemaphoreType.DMA((4,)),
        ],
        compiler_params=pltpu.CompilerParams(
            collective_id=0, has_side_effects=True, vmem_limit_bytes=63 * 1024 * 1024
        ),
    )(
        tokens, token_job_index.reshape(1, JOB_ROWS), jnp.swapaxes(gate_up, 1, 2), down,
        adapter_in, jnp.swapaxes(adapter_out, 1, 2), cotangent.T,
    )
    dma = pltpu.SemaphoreType.DMA((10,))
    mixed, grad, grad_in, grad_out = pl.pallas_call(
        hand_over,
        out_shape=[jax.ShapeDtypeStruct(out.shape, out.dtype) for out in outs],
        in_specs=[hbm] * 4,
        out_specs=[hbm] * 4,
        scratch_shapes=[buf(out.shape, out.dtype) for out in outs] + [dma, dma],
        compiler_params=pltpu.CompilerParams(vmem_limit_bytes=63 * 1024 * 1024),
    )(*outs)
    return mixed.T, grad.T, grad_in, jnp.swapaxes(grad_out, 1, 2)


def solution(mesh):
    return jax.shard_map(
        local,
        mesh=mesh,
        in_specs=(
            P("dp", "width"),
            P("dp"),
            P(None, "width", ("dp", "hidden")),
            P(("dp", "hidden"), "width"),
            P(None, "width", None),
            P(None, None, ("dp", "hidden")),
            P("dp", ("width", "hidden")),
        ),
        out_specs=(
            P("dp", ("width", "hidden")),
            P("dp", ("width", "hidden")),
            P(None, "width", None),
            P(None, None, ("dp", "hidden")),
        ),
        check_vma=False,
    )
```
